32 devices in a mesh: dcp: 8 (over z, y), rep: 4 (over x, core).
Axes of the slice: x: 2, y: 2, z: 4, core: 2. Of those that a mesh axis runs over, the one named last changes fastest.
Arguments:
- query: bfloat16 [4096, 1024], P(('rep', 'dcp')), parts along dimension 0, may hold values from -6 to 6
- key: bfloat16 [4096, 128], P(('rep', 'dcp')), parts along dimension 0, may hold values from -6 to 6
- value: bfloat16 [4096, 128], P(('rep', 'dcp')), parts along dimension 0, may hold values from -6 to 6
- grad_out: bfloat16 [4096, 1024], P(('rep', 'dcp')), parts along dimension 0, may hold values from -6 to 6
- loader_pos: int32 [4096], P('rep'), parts along dimension 0, may hold values from 0 to 1023, as said below
- doc_lengths: int32 [12], P('rep'), parts along dimension 0, may hold values from 1 to 640, 1024 in all
Outputs:
- attn_out: bfloat16 [4096, 1024], P(('rep', 'dcp')), parts along dimension 0
- dquery: bfloat16 [4096, 1024], P(('rep', 'dcp')), parts along dimension 0
- dkey: bfloat16 [4096, 128], P(('rep', 'dcp')), parts along dimension 0
- dvalue: bfloat16 [4096, 128], P(('rep', 'dcp')), parts along dimension 0
The draws below stay inside these ranges and needn't reach their ends.
There are 4 independent parts, one for each index of `rep`. The reference program is written for one: setup_inputs(seed, part) draws one part's arguments, and reference() takes and returns one part's arrays. A program takes and returns all parts, laid end to end along the dimension named above; each array names one. Nothing has to cross between parts.
Inputs may be any that keep to these rules, and one draw needn't show every extreme that they name: `loader_pos`: a permutation of the 1024 context positions; each aligned block of 128 loader rows holds exactly 128 // 8 positions of every aligned block of 128 context positions.
All inputs are finite; a program needn't handle non-finite values.
Results may differ from the reference program's by a relative error of at most 0.023.
Values may be sent and summed in bfloat16 or wider, within the bound.
No kernel may reach another device: no remote copies, remote signals or barrier semaphores. Data moves between devices by JAX's collectives and lax.ppermute only.
A program may use at most 64 MiB of HBM per device.

```python
import math
import jax
import jax.numpy as jnp
import numpy as np
from jax import lax

HEADS = 8
DH = 128
TOK_DEV = 128
SPAN = 5
TOKENS = 1024
MAXDOC = 640
NDOCS = 3


def loader_positions(key):
    key = jax.random.fold_in(key, 11)
    blocks = TOKENS // TOK_DEV
    per_peer = TOK_DEV // blocks
    first_key, second_key = jax.random.split(key)
    spread = jax.vmap(lambda subkey: jax.random.permutation(subkey, TOK_DEV))(jax.random.split(first_key, blocks))
    spread = spread.astype(jnp.int32) + (jnp.arange(blocks, dtype=jnp.int32) * TOK_DEV)[:, None]
    spread = spread.reshape(blocks, blocks, per_peer).transpose(1, 0, 2).reshape(blocks, TOK_DEV)
    shuffle = jax.vmap(lambda subkey: jax.random.permutation(subkey, TOK_DEV))(jax.random.split(second_key, blocks))
    spread = jnp.take_along_axis(spread, shuffle.astype(jnp.int32), axis=1)
    return spread.reshape(TOKENS).astype(jnp.int32)


def draw_loader_pos(key, part):
    return loader_positions(key)


def draw_query(key, part):
    positions = loader_positions(key)
    key = jax.random.fold_in(key, 21)
    noise = jax.random.truncated_normal(key, -4.0, 4.0, (TOKENS, HEADS * DH), jnp.float32)
    return noise[positions].astype(jnp.bfloat16)


def draw_key(key, part):
    positions = loader_positions(key)
    key = jax.random.fold_in(key, 22)
    noise = jax.random.truncated_normal(key, -4.0, 4.0, (TOKENS, DH), jnp.float32)
    return noise[positions].astype(jnp.bfloat16)


def steps_of(own_key, dims, shards, least, top_value):
    level, own = 1.0, jax.random.fold_in(own_key, 6)
    for position, parts in shards:
        steps = jnp.exp(jax.random.uniform(jax.random.fold_in(own, position), (parts,), jnp.float32, least / len(shards), top_value / len(shards)))
        level = level * jnp.repeat(steps, dims[position] // parts).reshape([-1 if axis == position else 1 for axis in range(len(dims))])
    return level


def split_up(amount, total, reach, lean):
    weights = [(1 << 20) // math.isqrt(rank ** lean) + 1 for rank in range(2, amount + 1)]
    rest, counts = total - reach - (amount - 1), [1] * (amount - 1)
    while rest > 0:
        movable = [i for i in range(amount - 1) if counts[i] < reach]
        whole, left = sum([weights[i] for i in movable]), rest
        for i in movable:
            addition = min(reach - counts[i], max(1, left * weights[i] // whole), rest)
            counts[i] = counts[i] + addition
            rest = rest - addition
    return np.array([reach] + counts)


def uneven_parts(own_key, amount, total, most, lean):
    if amount == 2:
        one = jax.random.randint(own_key, (), max(1, total - most), min(most, total - 1) + 1)
        return jnp.stack([one, total - one])
    lengths = jnp.asarray(split_up(amount, total, most, lean), jnp.int32)
    couples = (amount - 1) // 2
    giver, sink = lengths[1:1 + 2 * couples:2], lengths[2:2 + 2 * couples:2]
    slack = jnp.minimum(giver - 1, most - sink)
    passed = jax.random.randint(jax.random.fold_in(own_key, 1), (couples,), 0, 1 << 20) % (slack + 1)
    lengths = lengths.at[1:1 + 2 * couples:2].set(giver - passed).at[2:2 + 2 * couples:2].set(sink + passed)
    return lengths[jax.random.permutation(jax.random.fold_in(own_key, 2), amount)]


def gaussian(stream_key, shape, scale, most, cuts=(), kind=jnp.bfloat16):
    array = jax.random.normal(stream_key, shape, jnp.float32) * scale
    if len(cuts) > 0:
        array = steps_of(stream_key, shape, cuts, -0.22, 0.18) * array
    return jnp.clip(array, min=-most, max=most).astype(kind)


def setup_inputs(seed: int = 0, part: int = 0) -> dict:
    arg_keys = jax.random.split(jax.random.key(seed), 7)
    part_keys = jax.random.split(jax.random.fold_in(arg_keys[6], part), 7)
    query = draw_query(jax.random.fold_in(jax.random.fold_in(arg_keys[6], part), 71), part)
    key = draw_key(jax.random.fold_in(jax.random.fold_in(arg_keys[6], part), 71), part)
    value = gaussian(part_keys[2], (TOKENS, DH), 1.0, 6.0, ((0, 8),))
    grad_out = gaussian(part_keys[3], (TOKENS, HEADS * DH), 1.0, 6.0, ((0, 8),))
    loader_pos = draw_loader_pos(jax.random.fold_in(jax.random.fold_in(arg_keys[6], part), 71), part)
    doc_lengths = uneven_parts(part_keys[5], NDOCS, TOKENS, MAXDOC, 2).astype(jnp.int32)
    return dict(query=query, key=key, value=value, grad_out=grad_out, loader_pos=loader_pos, doc_lengths=doc_lengths)


def document_of(positions, doc_lengths):
    doc_ends = jnp.cumsum(doc_lengths)
    return lax.optimization_barrier(jnp.sum((positions[:, None] >= doc_ends[None, :]).astype(jnp.int32), axis=1))

def reference(query, key, value, grad_out, loader_pos, doc_lengths):
    score_scale = 1.0 / math.sqrt(DH)
    inverse = jnp.zeros((TOKENS,), jnp.int32).at[loader_pos].set(jnp.arange(TOKENS, dtype=jnp.int32))
    ctx_query = query[inverse]
    ctx_grad = grad_out[inverse]
    ctx_pairs = jnp.concatenate([key[inverse], value[inverse]], axis=1)
    window_span = SPAN * TOK_DEV
    padded = jnp.concatenate([jnp.zeros((window_span, 2 * DH), jnp.bfloat16), ctx_pairs], axis=0)
    slot_ids = jnp.arange(TOK_DEV, dtype=jnp.int32)
    window_ids = jnp.arange(window_span + TOK_DEV, dtype=jnp.int32)

    def query_block(running, block_index):
        first_row = block_index * TOK_DEV
        queries = lax.dynamic_slice_in_dim(ctx_query, first_row, TOK_DEV, 0).reshape(TOK_DEV, HEADS, DH).astype(jnp.float32)
        grad_rows = lax.dynamic_slice_in_dim(ctx_grad, first_row, TOK_DEV, 0).reshape(TOK_DEV, HEADS, DH).astype(jnp.float32)
        window = lax.dynamic_slice_in_dim(padded, first_row, window_span + TOK_DEV, 0).astype(jnp.float32)
        key_rows = window[:, :DH]
        value_rows = window[:, DH:]
        query_pos = first_row + slot_ids
        key_pos = first_row - window_span + window_ids
        allowed = (key_pos[None, :] >= 0) & (key_pos[None, :] <= query_pos[:, None])
        allowed = allowed & (document_of(query_pos, doc_lengths)[:, None] == document_of(key_pos, doc_lengths)[None, :])
        scores = jnp.einsum('qhd,kd->hqk', queries, key_rows) * score_scale
        masked = jnp.where(allowed[None], scores, -jnp.inf)
        row_top = lax.optimization_barrier(jnp.max(masked, axis=2, keepdims=True))
        row_total = lax.optimization_barrier(jnp.sum(jnp.where(allowed[None], jnp.exp(scores - row_top), 0.0), axis=2, keepdims=True))
        log_total = row_top + jnp.log(row_total)
        prob_full = jnp.where(allowed[None], jnp.exp(scores - log_total), 0.0)
        prob_low = lax.optimization_barrier(prob_full.astype(jnp.bfloat16)).astype(jnp.float32)
        attended = jnp.einsum('hqk,kd->qhd', prob_low, value_rows).astype(jnp.bfloat16)
        row_delta = jnp.einsum('qhd,qhd->hq', grad_rows, attended.astype(jnp.float32))
        grad_prob = jnp.einsum('qhd,kd->hqk', grad_rows, value_rows)
        grad_score = (prob_full * (grad_prob - row_delta[:, :, None])).astype(jnp.bfloat16)
        grad_score = lax.optimization_barrier(grad_score).astype(jnp.float32)
        grad_query = (jnp.einsum('hqk,kd->qhd', grad_score, key_rows) * score_scale).astype(jnp.bfloat16)
        grad_key = jnp.einsum('hqk,qhd->kd', grad_score, queries) * score_scale
        grad_value = jnp.einsum('hqk,qhd->kd', prob_low, grad_rows)
        update = jnp.concatenate([grad_key, grad_value], axis=1)
        current = lax.dynamic_slice_in_dim(running, first_row, window_span + TOK_DEV, 0)
        running = lax.dynamic_update_slice_in_dim(running, current + update, first_row, 0)
        return (running, (attended.reshape(TOK_DEV, HEADS * DH), grad_query.reshape(TOK_DEV, HEADS * DH)))
    initial = jnp.zeros((window_span + TOKENS, 2 * DH), jnp.float32)
    finished, outputs = lax.scan(query_block, initial, jnp.arange(TOKENS // TOK_DEV, dtype=jnp.int32))
    attended_all = outputs[0].reshape(TOKENS, HEADS * DH)
    grad_query_all = outputs[1].reshape(TOKENS, HEADS * DH)
    key_grads = finished[window_span:]
    return (attended_all, grad_query_all, key_grads[:, :DH].astype(jnp.bfloat16), key_grads[:, DH:].astype(jnp.bfloat16))
```

```python
import functools
import math

import jax
import jax.numpy as jnp
from jax import lax
from jax.experimental import pallas as pl
from jax.experimental.pallas import tpu as pltpu
from jax.sharding import PartitionSpec as P

SPAN = 5
LANES = 128
NEG = -1e30
F32 = jnp.float32
BF16 = jnp.bfloat16


def dot(a, b, dims):
    return lax.dot_general(a, b, (dims, ((), ())), preferred_element_type=F32)


def pack_kernel(per_peer, pos_ref, q_ref, k_ref, v_ref, g_ref, out_ref):
    tok, width = q_ref.shape
    head = k_ref.shape[1]
    me = lax.axis_index("dcp")
    pos_row = pos_ref[pl.ds(me, 1), :]
    pos_col = jnp.transpose(jnp.broadcast_to(pos_row, (tok, tok)))
    smaller = (pos_col < pos_row).astype(jnp.int32)
    rank = jnp.sum(smaller, axis=0, keepdims=True)
    slot = jnp.broadcast_to((pos_row % tok).astype(F32), (tok, tok))
    want = lax.broadcasted_iota(jnp.int32, (tok, tok), 0)
    lane = lax.broadcasted_iota(jnp.int32, (tok, LANES), 1)
    perm = (rank == want).astype(BF16)
    out_ref[:, :width] = dot(perm, q_ref[...], ((1,), (0,))).astype(BF16)
    out_ref[:, width : 2 * width] = dot(perm, g_ref[...], ((1,), (0,))).astype(BF16)
    slots = jnp.zeros((tok, LANES), F32)
    for block in range(SPAN + 1):
        chosen = rank == want + (block - SPAN) * per_peer
        perm = chosen.astype(BF16)
        first = 2 * width + 2 * head * block
        out_ref[:, first : first + head] = dot(perm, k_ref[...], ((1,), (0,))).astype(BF16)
        out_ref[:, first + head : first + 2 * head] = dot(perm, v_ref[...], ((1,), (0,))).astype(BF16)
        column = jnp.sum(jnp.where(chosen, slot, 0.0), axis=1, keepdims=True)
        slots = jnp.where(lane == block, column, slots)
    first = 2 * width + 2 * head * (SPAN + 1)
    out_ref[:, first : first + LANES] = slots.astype(BF16)


def attend_kernel(width, head, len_ref, in_ref, attn_ref, dq_ref, own_ref, *part_refs):
    tok = in_ref.shape[0]
    heads = width // head
    me = lax.axis_index("dcp")
    scale = 1.0 / math.sqrt(head)
    factor = scale * math.log2(math.e)
    base = 2 * width
    slots = in_ref[:, base + 2 * head * (SPAN + 1) :].astype(F32)
    target = lax.broadcasted_iota(jnp.int32, (tok, tok), 1).astype(F32)
    keys, values = [], []
    place = None
    for block in range(SPAN + 1):
        place = (slots[:, block : block + 1] == target).astype(BF16)
        first = base + 2 * head * block
        both = dot(place, in_ref[:, first : first + 2 * head], ((0,), (0,))).astype(BF16)
        keys.append(both[:, :head])
        values.append(both[:, head:])
    key = jnp.concatenate(keys, axis=0)
    value = jnp.concatenate(values, axis=0)
    queries = dot(place, in_ref[:, :width], ((0,), (0,))).astype(BF16)
    grads = dot(place, in_ref[:, width:base], ((0,), (0,))).astype(BF16)

    pairs = 2
    cols = pairs * tok
    window = (SPAN + 1) * tok
    lane = lax.broadcasted_iota(jnp.int32, (1, cols), 1)
    q_pos = me * tok + lane % tok
    q_start = jnp.zeros((1, cols), jnp.int32)
    end = jnp.int32(0)
    for doc in range(len_ref.shape[0]):
        end = end + len_ref[doc]
        q_start = jnp.where(q_pos >= end, end, q_start)
    k_pos = (me - SPAN) * tok + lax.broadcasted_iota(jnp.int32, (window, cols), 0)
    allowed = (k_pos >= q_start) & (k_pos <= q_pos)

    key_grad = jnp.zeros((window, head), F32)
    value_grad = jnp.zeros((window, head), F32)
    for first in range(0, heads, pairs):
        spans = [slice(h * head, (h + 1) * head) for h in range(first, first + pairs)]
        q_two = jnp.concatenate([queries[:, s] for s in spans], axis=0)
        g_two = jnp.concatenate([grads[:, s] for s in spans], axis=0)
        scores = jnp.where(allowed, dot(key, q_two, ((1,), (1,))), NEG)
        top = jnp.max(scores, axis=0, keepdims=True)
        weights = jnp.exp2((scores - top) * factor)
        inverse = 1.0 / jnp.sum(weights, axis=0, keepdims=True)
        prob = weights * inverse
        prob_low = prob.astype(BF16)
        grad_prob = dot(value, g_two, ((1,), (1,)))
        delta = jnp.sum(prob * grad_prob, axis=0, keepdims=True)
        grad_score = (prob * (grad_prob - delta)).astype(BF16)
        value_grad += dot(prob_low, g_two, ((1,), (0,)))
        key_grad += dot(grad_score, q_two, ((1,), (0,)))
        out_t = dot(value, prob_low, ((0,), (0,)))
        dq_t = dot(key, grad_score, ((0,), (0,))) * scale
        for i, s in enumerate(spans):
            attn_ref[:, s] = jnp.transpose(out_t[:, i * tok : (i + 1) * tok]).astype(BF16)
            dq_ref[:, s] = jnp.transpose(dq_t[:, i * tok : (i + 1) * tok]).astype(BF16)
    key_grad = key_grad * scale
    own_ref[:, :head] = key_grad[SPAN * tok :, :]
    own_ref[:, head:] = value_grad[SPAN * tok :, :]
    for offset in range(1, SPAN + 1):
        rows = slice((SPAN - offset) * tok, (SPAN - offset + 1) * tok)
        part_refs[offset - 1][:, :head] = key_grad[rows, :].astype(BF16)
        part_refs[offset - 1][:, head:] = value_grad[rows, :].astype(BF16)


def per_device(query, key, value, grad_out, loader_pos, doc_lengths):
    tok, width = query.shape
    head = key.shape[1]
    devices = lax.axis_size("dcp")
    per_peer = tok // devices
    vmem = pl.BlockSpec(memory_space=pltpu.VMEM)
    smem = pl.BlockSpec(memory_space=pltpu.SMEM)
    params = pltpu.CompilerParams(vmem_limit_bytes=48 << 20)
    total = 2 * width + 2 * head * (SPAN + 1) + LANES
    packed = pl.pallas_call(
        functools.partial(pack_kernel, per_peer),
        out_shape=jax.ShapeDtypeStruct((tok, total), BF16),
        in_specs=[vmem] * 5,
        out_specs=vmem,
        compiler_params=params,
        name="pack",
    )(loader_pos.reshape(devices, tok), query, key, value, grad_out)
    arrived = lax.all_to_all(packed, "dcp", split_axis=0, concat_axis=0, tiled=True)
    wide = jax.ShapeDtypeStruct((tok, width), BF16)
    part = jax.ShapeDtypeStruct((tok, 2 * head), BF16)
    attn_out, dquery, summed, *parts = pl.pallas_call(
        functools.partial(attend_kernel, width, head),
        out_shape=[wide, wide, jax.ShapeDtypeStruct((tok, 2 * head), F32)] + [part] * SPAN,
        in_specs=[smem, vmem],
        out_specs=[vmem] * (3 + SPAN),
        compiler_params=params,
        name="attend",
    )(doc_lengths, arrived)
    for offset in range(1, SPAN + 1):
        pairs = [(source, source - offset) for source in range(offset, devices)]
        summed = summed + lax.ppermute(parts[offset - 1], "dcp", pairs).astype(F32)
    return attn_out, dquery, summed[:, :head].astype(BF16), summed[:, head:].astype(BF16)


def solution(mesh):
    rows = P(("rep", "dcp"), None)
    return jax.shard_map(
        per_device,
        mesh=mesh,
        in_specs=(rows, rows, rows, rows, P("rep"), P("rep")),
        out_specs=(rows, rows, rows, rows),
        check_vma=False,
    )
```

```python
import functools
import math

import jax
import jax.numpy as jnp
from jax import lax
from jax.experimental import pallas as pl
from jax.experimental.pallas import tpu as pltpu
from jax.sharding import PartitionSpec as P

SPAN = 5
LANES = 128
NEG = -1e30
F32 = jnp.float32
BF16 = jnp.bfloat16


def dot(a, b, dims):
    return lax.dot_general(a, b, (dims, ((), ())), preferred_element_type=F32)


def pack_kernel(
    per_peer, pos_hbm, len_hbm, q_hbm, k_hbm, v_hbm, g_hbm, out_ref, slot_ref, start_ref,
    pos_ref, len_ref, q_ref, k_ref, v_ref, g_ref, sems,
):
    sources = (pos_hbm, len_hbm, k_hbm, v_hbm, q_hbm, g_hbm)
    targets = (pos_ref, len_ref, k_ref, v_ref, q_ref, g_ref)
    copies = [
        pltpu.make_async_copy(source, target, sems.at[i])
        for i, (source, target) in enumerate(zip(sources, targets))
    ]
    for copy in copies:
        copy.start()
    tok, width = q_ref.shape
    head = k_ref.shape[1]
    devices = pos_ref.shape[0]
    me = lax.axis_index("dcp")
    want = lax.broadcasted_iota(jnp.int32, (tok, tok), 0)
    copies[0].wait()

    def rank_of(device):
        pos_row = pos_ref[pl.ds(device, 1), :]
        pos_col = jnp.transpose(jnp.broadcast_to(pos_row, (tok, tok)))
        return pos_row, jnp.sum((pos_col < pos_row).astype(jnp.int32), axis=0, keepdims=True)

    rows = (SPAN + 1) * per_peer
    window = (me - SPAN) * per_peer + lax.broadcasted_iota(jnp.int32, (rows, tok), 0)
    lane = lax.broadcasted_iota(jnp.int32, (per_peer, LANES), 1)

    def slots_from(source):
        pos_row, rank = rank_of(source)
        slot = (pos_row % tok).astype(F32)
        column = jnp.sum(jnp.where(rank == window, slot, 0.0), axis=1, keepdims=True)
        slots = jnp.zeros((per_peer, LANES), F32)
        for block in range(SPAN + 1):
            slots = jnp.where(lane == block, column[block * per_peer : (block + 1) * per_peer], slots)
        return slots

    if devices <= 16:
        for source in range(devices):
            slot_ref[source * per_peer : (source + 1) * per_peer, :] = slots_from(source)
    else:

        @pl.loop(0, devices)
        def _(source):
            slot_ref[pl.ds(source * per_peer, per_peer), :] = slots_from(source)

    copies[1].wait()
    q_pos = me * tok + lax.broadcasted_iota(jnp.int32, start_ref.shape, 1) % tok
    q_start = jnp.zeros(start_ref.shape, jnp.int32)
    end = jnp.int32(0)
    for doc in range(len_ref.shape[0]):
        end = end + len_ref[doc]
        q_start = jnp.where(q_pos >= end, end, q_start)
    start_ref[...] = q_start

    _, rank = rank_of(me)
    copies[2].wait()
    copies[3].wait()
    for block in range(SPAN + 1):
        perm = (rank == want + (block - SPAN) * per_peer).astype(BF16)
        first = 2 * width + 2 * head * block
        out_ref[:, first : first + head] = dot(perm, k_ref[...], ((1,), (0,))).astype(BF16)
        out_ref[:, first + head : first + 2 * head] = dot(perm, v_ref[...], ((1,), (0,))).astype(BF16)
    perm = (rank == want).astype(BF16)
    copies[4].wait()
    out_ref[:, :width] = dot(perm, q_ref[...], ((1,), (0,))).astype(BF16)
    copies[5].wait()
    out_ref[:, width : 2 * width] = dot(perm, g_ref[...], ((1,), (0,))).astype(BF16)


def attend_kernel(width, head, start_ref, slot_ref, in_ref, attn_ref, dq_ref, own_ref, *part_refs):
    tok = in_ref.shape[0]
    heads = width // head
    me = lax.axis_index("dcp")
    scale = 1.0 / math.sqrt(head)
    factor = scale * math.log2(math.e)
    base = 2 * width
    slots = slot_ref[...]
    target = lax.broadcasted_iota(jnp.int32, (tok, tok), 1).astype(F32)
    keys, values = [], []
    place = None
    for block in range(SPAN + 1):
        place = (slots[:, block : block + 1] == target).astype(BF16)
        first = base + 2 * head * block
        both = dot(place, in_ref[:, first : first + 2 * head], ((0,), (0,))).astype(BF16)
        keys.append(both[:, :head])
        values.append(both[:, head:])
    key = jnp.concatenate(keys, axis=0)
    value = jnp.concatenate(values, axis=0)
    queries = dot(place, in_ref[:, :width], ((0,), (0,))).astype(BF16)
    grads = dot(place, in_ref[:, width:base], ((0,), (0,))).astype(BF16)

    pairs = 2
    cols = pairs * tok
    window = (SPAN + 1) * tok
    lane = lax.broadcasted_iota(jnp.int32, (1, cols), 1)
    q_pos = me * tok + lane % tok
    q_start = start_ref[:1, :]
    k_pos = (me - SPAN) * tok + lax.broadcasted_iota(jnp.int32, (window, cols), 0)
    allowed = (k_pos >= q_start) & (k_pos <= q_pos)

    key_grad = jnp.zeros((window, head), F32)
    value_grad = jnp.zeros((window, head), F32)
    for first in range(0, heads, pairs):
        spans = [slice(h * head, (h + 1) * head) for h in range(first, first + pairs)]
        q_two = jnp.concatenate([queries[:, s] for s in spans], axis=0)
        g_two = jnp.concatenate([grads[:, s] for s in spans], axis=0)
        scores = jnp.where(allowed, dot(key, q_two, ((1,), (1,))), NEG)
        top = jnp.max(scores, axis=0, keepdims=True)
        weights = jnp.exp2((scores - top) * factor)
        inverse = 1.0 / jnp.sum(weights, axis=0, keepdims=True)
        prob = weights * inverse
        prob_low = prob.astype(BF16)
        grad_prob = dot(value, g_two, ((1,), (1,)))
        delta = jnp.sum(prob * grad_prob, axis=0, keepdims=True)
        grad_score = (prob * (grad_prob - delta)).astype(BF16)
        value_grad += dot(prob_low, g_two, ((1,), (0,)))
        key_grad += dot(grad_score, q_two, ((1,), (0,)))
        out_t = dot(value, prob_low, ((0,), (0,)))
        dq_t = dot(key, grad_score, ((0,), (0,))) * scale
        for i, s in enumerate(spans):
            attn_ref[:, s] = jnp.transpose(out_t[:, i * tok : (i + 1) * tok]).astype(BF16)
            dq_ref[:, s] = jnp.transpose(dq_t[:, i * tok : (i + 1) * tok]).astype(BF16)
    key_grad = key_grad * scale
    own_ref[:, :head] = key_grad[SPAN * tok :, :]
    own_ref[:, head:] = value_grad[SPAN * tok :, :]
    for offset in range(1, SPAN + 1):
        rows = slice((SPAN - offset) * tok, (SPAN - offset + 1) * tok)
        part_refs[offset - 1][:, :head] = key_grad[rows, :].astype(BF16)
        part_refs[offset - 1][:, head:] = value_grad[rows, :].astype(BF16)


def per_device(query, key, value, grad_out, loader_pos, doc_lengths):
    tok, width = query.shape
    head = key.shape[1]
    devices = lax.axis_size("dcp")
    per_peer = tok // devices
    vmem = pl.BlockSpec(memory_space=pltpu.VMEM)
    params = pltpu.CompilerParams(vmem_limit_bytes=48 << 20)
    hbm = pl.BlockSpec(memory_space=pltpu.HBM)
    total = 2 * width + 2 * head * (SPAN + 1)
    packed, slots, starts = pl.pallas_call(
        functools.partial(pack_kernel, per_peer),
        out_shape=[
            jax.ShapeDtypeStruct((tok, total), BF16),
            jax.ShapeDtypeStruct((tok, LANES), F32),
            jax.ShapeDtypeStruct((8, 2 * tok), jnp.int32),
        ],
        in_specs=[hbm] * 6,
        out_specs=[vmem] * 3,
        scratch_shapes=[
            pltpu.VMEM((devices, tok), jnp.int32),
            pltpu.SMEM(doc_lengths.shape, jnp.int32),
            pltpu.VMEM(query.shape, BF16),
            pltpu.VMEM(key.shape, BF16),
            pltpu.VMEM(value.shape, BF16),
            pltpu.VMEM(grad_out.shape, BF16),
            pltpu.SemaphoreType.DMA((6,)),
        ],
        compiler_params=params,
        name="pack",
    )(loader_pos.reshape(devices, tok), doc_lengths, query, key, value, grad_out)
    arrived = lax.all_to_all(packed, "dcp", split_axis=0, concat_axis=0, tiled=True)
    wide = jax.ShapeDtypeStruct((tok, width), BF16)
    part = jax.ShapeDtypeStruct((tok, 2 * head), BF16)
    attn_out, dquery, summed, *parts = pl.pallas_call(
        functools.partial(attend_kernel, width, head),
        out_shape=[wide, wide, jax.ShapeDtypeStruct((tok, 2 * head), F32)] + [part] * SPAN,
        in_specs=[vmem] * 3,
        out_specs=[vmem] * (3 + SPAN),
        compiler_params=params,
        name="attend",
    )(starts, slots, arrived)
    for offset in (4, 5, 3, 2, 1):
        pairs = [(source, source - offset) for source in range(offset, devices)]
        summed = summed + lax.ppermute(parts[offset - 1], "dcp", pairs).astype(F32)
    return attn_out, dquery, summed[:, :head].astype(BF16), summed[:, head:].astype(BF16)


def solution(mesh):
    rows = P(("rep", "dcp"), None)
    return jax.shard_map(
        per_device,
        mesh=mesh,
        in_specs=(rows, rows, rows, rows, P("rep"), P("rep")),
        out_specs=(rows, rows, rows, rows),
        check_vma=False,
    )
```

```python
import functools
import math

import jax
import jax.numpy as jnp
from jax import lax
from jax.experimental import pallas as pl
from jax.experimental.pallas import tpu as pltpu
from jax.sharding import PartitionSpec as P

SPAN = 5
LANES = 128
NEG = -1e30
F32 = jnp.float32
BF16 = jnp.bfloat16


def dot(a, b, dims):
    return lax.dot_general(a, b, (dims, ((), ())), preferred_element_type=F32)


def pack_kernel(
    per_peer, pos_hbm, len_hbm, q_hbm, k_hbm, v_hbm, g_hbm, out_ref, slot_ref, start_ref,
    pos_ref, len_ref, q_ref, k_ref, v_ref, g_ref, sems,
):
    sources = (pos_hbm, len_hbm, k_hbm, v_hbm, q_hbm, g_hbm)
    targets = (pos_ref, len_ref, k_ref, v_ref, q_ref, g_ref)
    copies = [
        pltpu.make_async_copy(source, target, sems.at[i])
        for i, (source, target) in enumerate(zip(sources, targets))
    ]
    for copy in copies:
        copy.start()
    tok, width = q_ref.shape
    head = k_ref.shape[1]
    devices = pos_ref.shape[0]
    me = lax.axis_index("dcp")
    want = lax.broadcasted_iota(jnp.int32, (tok, tok), 0)
    copies[0].wait()

    def rank_of(device):
        pos_row = pos_ref[pl.ds(device, 1), :]
        pos_col = jnp.transpose(jnp.broadcast_to(pos_row, (tok, tok)))
        return pos_row, jnp.sum((pos_col < pos_row).astype(jnp.int32), axis=0, keepdims=True)

    rows = (SPAN + 1) * per_peer
    window = (me - SPAN) * per_peer + lax.broadcasted_iota(jnp.int32, (rows, tok), 0)
    lane = lax.broadcasted_iota(jnp.int32, (per_peer, LANES), 1)

    def slots_from(source):
        pos_row, rank = rank_of(source)
        slot = (pos_row % tok).astype(F32)
        column = jnp.sum(jnp.where(rank == window, slot, 0.0), axis=1, keepdims=True)
        slots = jnp.zeros((per_peer, LANES), F32)
        for block in range(SPAN + 1):
            slots = jnp.where(lane == block, column[block * per_peer : (block + 1) * per_peer], slots)
        return slots

    if devices <= 16:
        for source in range(devices):
            slot_ref[source * per_peer : (source + 1) * per_peer, :] = slots_from(source)
    else:

        @pl.loop(0, devices)
        def _(source):
            slot_ref[pl.ds(source * per_peer, per_peer), :] = slots_from(source)

    copies[1].wait()
    q_pos = me * tok + lax.broadcasted_iota(jnp.int32, start_ref.shape, 1) % tok
    q_start = jnp.zeros(start_ref.shape, jnp.int32)
    end = jnp.int32(0)
    for doc in range(len_ref.shape[0]):
        end = end + len_ref[doc]
        q_start = jnp.where(q_pos >= end, end, q_start)
    start_ref[...] = q_start

    _, rank = rank_of(me)
    copies[2].wait()
    copies[3].wait()
    for block in range(SPAN + 1):
        perm = (rank == want + (block - SPAN) * per_peer).astype(BF16)
        first = 2 * width + 2 * head * block
        out_ref[:, first : first + head] = dot(perm, k_ref[...], ((1,), (0,))).astype(BF16)
        out_ref[:, first + head : first + 2 * head] = dot(perm, v_ref[...], ((1,), (0,))).astype(BF16)
    perm = (rank == want).astype(BF16)
    copies[4].wait()
    out_ref[:, :width] = dot(perm, q_ref[...], ((1,), (0,))).astype(BF16)
    copies[5].wait()
    out_ref[:, width : 2 * width] = dot(perm, g_ref[...], ((1,), (0,))).astype(BF16)


def attend_kernel(width, head, start_ref, slot_ref, in_ref, attn_ref, dq_ref, own_ref, *part_refs):
    tok = in_ref.shape[0]
    heads = width // head
    me = lax.axis_index("dcp")
    scale = 1.0 / math.sqrt(head)
    factor = scale * math.log2(math.e)
    base = 2 * width
    slots = slot_ref[...]
    target = lax.broadcasted_iota(jnp.int32, (tok, tok), 1).astype(F32)
    keys, values = [], []
    place = None
    for block in range(SPAN + 1):
        place = (slots[:, block : block + 1] == target).astype(BF16)
        first = base + 2 * head * block
        both = dot(place, in_ref[:, first : first + 2 * head], ((0,), (0,))).astype(BF16)
        keys.append(both[:, :head])
        values.append(both[:, head:])
    key = jnp.concatenate(keys, axis=0)
    value = jnp.concatenate(values, axis=0)
    queries = dot(place, in_ref[:, :width], ((0,), (0,))).astype(BF16)
    grads = dot(place, in_ref[:, width:base], ((0,), (0,))).astype(BF16)

    pairs = 2
    cols = pairs * tok
    window = (SPAN + 1) * tok
    lane = lax.broadcasted_iota(jnp.int32, (1, cols), 1)
    q_pos = me * tok + lane % tok
    q_start = start_ref[:1, :]
    k_pos = (me - SPAN) * tok + lax.broadcasted_iota(jnp.int32, (window, cols), 0)
    allowed = (k_pos >= q_start) & (k_pos <= q_pos)

    key_grad = jnp.zeros((window, head), F32)
    value_grad = jnp.zeros((window, head), F32)
    for first in range(0, heads, pairs):
        spans = [slice(h * head, (h + 1) * head) for h in range(first, first + pairs)]
        q_two = jnp.concatenate([queries[:, s] for s in spans], axis=0)
        g_two = jnp.concatenate([grads[:, s] for s in spans], axis=0)
        scores = jnp.where(allowed, dot(key, q_two, ((1,), (1,))), NEG)
        top = jnp.max(scores, axis=0, keepdims=True)
        weights = jnp.exp2((scores - top) * factor)
        inverse = 1.0 / jnp.sum(weights, axis=0, keepdims=True)
        prob = weights * inverse
        prob_low = prob.astype(BF16)
        grad_prob = dot(value, g_two, ((1,), (1,)))
        delta = jnp.sum(prob * grad_prob, axis=0, keepdims=True)
        grad_score = (prob * (grad_prob - delta)).astype(BF16)
        value_grad += dot(prob_low, g_two, ((1,), (0,)))
        key_grad += dot(grad_score, q_two, ((1,), (0,)))
        out_t = dot(value, prob_low, ((0,), (0,)))
        dq_t = dot(key, grad_score, ((0,), (0,))) * scale
        for i, s in enumerate(spans):
            attn_ref[:, s] = jnp.transpose(out_t[:, i * tok : (i + 1) * tok]).astype(BF16)
            dq_ref[:, s] = jnp.transpose(dq_t[:, i * tok : (i + 1) * tok]).astype(BF16)
    key_grad = key_grad * scale
    own_ref[:, :head] = key_grad[SPAN * tok :, :]
    own_ref[:, head:] = value_grad[SPAN * tok :, :]
    for offset in range(1, SPAN + 1):
        rows = slice((SPAN - offset) * tok, (SPAN - offset + 1) * tok)
        part_refs[offset - 1][:, :head] = key_grad[rows, :].astype(BF16)
        part_refs[offset - 1][:, head:] = value_grad[rows, :].astype(BF16)


def per_device(query, key, value, grad_out, loader_pos, doc_lengths):
    tok, width = query.shape
    head = key.shape[1]
    devices = lax.axis_size("dcp")
    per_peer = tok // devices
    vmem = pl.BlockSpec(memory_space=pltpu.VMEM)
    params = pltpu.CompilerParams(vmem_limit_bytes=48 << 20)
    hbm = pl.BlockSpec(memory_space=pltpu.HBM)
    total = 2 * width + 2 * head * (SPAN + 1)
    packed, slots, starts = pl.pallas_call(
        functools.partial(pack_kernel, per_peer),
        out_shape=[
            jax.ShapeDtypeStruct((tok, total), BF16),
            jax.ShapeDtypeStruct((tok, LANES), F32),
            jax.ShapeDtypeStruct((8, 2 * tok), jnp.int32),
        ],
        in_specs=[hbm] * 6,
        out_specs=[vmem] * 3,
        scratch_shapes=[
            pltpu.VMEM((devices, tok), jnp.int32),
            pltpu.SMEM(doc_lengths.shape, jnp.int32),
            pltpu.VMEM(query.shape, BF16),
            pltpu.VMEM(key.shape, BF16),
            pltpu.VMEM(value.shape, BF16),
            pltpu.VMEM(grad_out.shape, BF16),
            pltpu.SemaphoreType.DMA((6,)),
        ],
        compiler_params=params,
        name="pack",
    )(*[pltpu.with_memory_space_constraint(x, pltpu.HBM) for x in (loader_pos.reshape(devices, tok), doc_lengths, query, key, value, grad_out)])
    arrived = lax.all_to_all(packed, "dcp", split_axis=0, concat_axis=0, tiled=True)
    wide = jax.ShapeDtypeStruct((tok, width), BF16)
    part = jax.ShapeDtypeStruct((tok, 2 * head), BF16)
    attn_out, dquery, summed, *parts = pl.pallas_call(
        functools.partial(attend_kernel, width, head),
        out_shape=[wide, wide, jax.ShapeDtypeStruct((tok, 2 * head), F32)] + [part] * SPAN,
        in_specs=[vmem] * 3,
        out_specs=[vmem] * (3 + SPAN),
        compiler_params=params,
        name="attend",
    )(starts, slots, arrived)
    for offset in (4, 5, 3, 2, 1):
        pairs = [(source, source - offset) for source in range(offset, devices)]
        summed = summed + lax.ppermute(parts[offset - 1], "dcp", pairs).astype(F32)
    return attn_out, dquery, summed[:, :head].astype(BF16), summed[:, head:].astype(BF16)


def solution(mesh):
    rows = P(("rep", "dcp"), None)
    return jax.shard_map(
        per_device,
        mesh=mesh,
        in_specs=(rows, rows, rows, rows, P("rep"), P("rep")),
        out_specs=(rows, rows, rows, rows),
        check_vma=False,
    )
```

```python
import functools
import math

import jax
import jax.numpy as jnp
from jax import lax
from jax.experimental import pallas as pl
from jax.experimental.pallas import tpu as pltpu
from jax.sharding import PartitionSpec as P

SPAN = 5
LANES = 128
NEG = -1e30
F32 = jnp.float32
BF16 = jnp.bfloat16


def dot(a, b, dims):
    return lax.dot_general(a, b, (dims, ((), ())), preferred_element_type=F32)


def pack_kernel(
    per_peer, paired, pos_hbm, len_hbm, q_hbm, k_hbm, v_hbm, g_hbm, *rest
):
    out_refs = rest[:-9]
    slot_ref, start_ref, pos_ref, len_ref, q_ref, k_ref, v_ref, g_ref, sems = rest[-9:]
    sources = (pos_hbm, len_hbm, k_hbm, v_hbm, q_hbm, g_hbm)
    targets = (pos_ref, len_ref, k_ref, v_ref, q_ref, g_ref)
    copies = [
        pltpu.make_async_copy(source, target, sems.at[i])
        for i, (source, target) in enumerate(zip(sources, targets))
    ]
    for copy in copies:
        copy.start()
    tok, width = q_ref.shape
    head = k_ref.shape[1]
    devices = pos_ref.shape[0]
    me = lax.axis_index("dcp")
    want = lax.broadcasted_iota(jnp.int32, (tok, tok), 0)
    if paired:
        want = ((want // per_peer) ^ me) * per_peer + want % per_peer
    copies[0].wait()

    def put(first, rows):
        rows = rows.astype(BF16)
        step = tok // len(out_refs)
        for i, out_ref in enumerate(out_refs):
            out_ref[:, first : first + rows.shape[1]] = rows[i * step : (i + 1) * step]

    def rank_of(device):
        pos_row = pos_ref[pl.ds(device, 1), :]
        pos_col = jnp.transpose(jnp.broadcast_to(pos_row, (tok, tok)))
        return pos_row, jnp.sum((pos_col < pos_row).astype(jnp.int32), axis=0, keepdims=True)

    rows = (SPAN + 1) * per_peer
    window = (me - SPAN) * per_peer + lax.broadcasted_iota(jnp.int32, (rows, tok), 0)
    lane = lax.broadcasted_iota(jnp.int32, (per_peer, LANES), 1)

    def slots_from(source):
        pos_row, rank = rank_of(source)
        slot = (pos_row % tok).astype(F32)
        column = jnp.sum(jnp.where(rank == window, slot, 0.0), axis=1, keepdims=True)
        slots = jnp.zeros((per_peer, LANES), F32)
        for block in range(SPAN + 1):
            slots = jnp.where(lane == block, column[block * per_peer : (block + 1) * per_peer], slots)
        return slots

    if devices <= 16:
        for source in range(devices):
            device = source ^ me if paired else source
            slot_ref[source * per_peer : (source + 1) * per_peer, :] = slots_from(device)
    else:

        @pl.loop(0, devices)
        def _(source):
            slot_ref[pl.ds(source * per_peer, per_peer), :] = slots_from(source)

    copies[1].wait()
    q_pos = me * tok + lax.broadcasted_iota(jnp.int32, start_ref.shape, 1) % tok
    q_start = jnp.zeros(start_ref.shape, jnp.int32)
    end = jnp.int32(0)
    for doc in range(len_ref.shape[0]):
        end = end + len_ref[doc]
        q_start = jnp.where(q_pos >= end, end, q_start)
    start_ref[...] = q_start

    _, rank = rank_of(me)
    copies[2].wait()
    copies[3].wait()
    for block in range(SPAN + 1):
        perm = (rank == want + (block - SPAN) * per_peer).astype(BF16)
        first = 2 * width + 2 * head * block
        put(first, dot(perm, k_ref[...], ((1,), (0,))))
        put(first + head, dot(perm, v_ref[...], ((1,), (0,))))
    perm = (rank == want).astype(BF16)
    copies[4].wait()
    put(0, dot(perm, q_ref[...], ((1,), (0,))))
    copies[5].wait()
    put(width, dot(perm, g_ref[...], ((1,), (0,))))


def attend_kernel(width, head, pieces, start_ref, slot_ref, *refs):
    in_refs = refs[:pieces]
    attn_ref, dq_ref, own_ref, *part_refs = refs[pieces:]
    tok = attn_ref.shape[0]
    heads = width // head
    me = lax.axis_index("dcp")
    scale = 1.0 / math.sqrt(head)
    factor = scale * math.log2(math.e)
    base = 2 * width
    slots = slot_ref[...]
    target = lax.broadcasted_iota(jnp.int32, (tok, tok), 1).astype(F32)

    def arrived(first, last):
        return jnp.concatenate([ref[:, first:last] for ref in in_refs], axis=0)

    keys, values = [], []
    place = None
    for block in range(SPAN + 1):
        place = (slots[:, block : block + 1] == target).astype(BF16)
        first = base + 2 * head * block
        both = dot(place, arrived(first, first + 2 * head), ((0,), (0,))).astype(BF16)
        keys.append(both[:, :head])
        values.append(both[:, head:])
    key = jnp.concatenate(keys, axis=0)
    value = jnp.concatenate(values, axis=0)
    queries = dot(place, arrived(0, width), ((0,), (0,))).astype(BF16)
    grads = dot(place, arrived(width, base), ((0,), (0,))).astype(BF16)

    pairs = 2
    cols = pairs * tok
    window = (SPAN + 1) * tok
    lane = lax.broadcasted_iota(jnp.int32, (1, cols), 1)
    q_pos = me * tok + lane % tok
    q_start = start_ref[:1, :]
    k_pos = (me - SPAN) * tok + lax.broadcasted_iota(jnp.int32, (window, cols), 0)
    allowed = (k_pos >= q_start) & (k_pos <= q_pos)

    key_grad = jnp.zeros((window, head), F32)
    value_grad = jnp.zeros((window, head), F32)
    for first in range(0, heads, pairs):
        spans = [slice(h * head, (h + 1) * head) for h in range(first, first + pairs)]
        q_two = jnp.concatenate([queries[:, s] for s in spans], axis=0)
        g_two = jnp.concatenate([grads[:, s] for s in spans], axis=0)
        scores = jnp.where(allowed, dot(key, q_two, ((1,), (1,))), NEG)
        top = jnp.max(scores, axis=0, keepdims=True)
        weights = jnp.exp2((scores - top) * factor)
        inverse = 1.0 / jnp.sum(weights, axis=0, keepdims=True)
        prob = weights * inverse
        prob_low = prob.astype(BF16)
        grad_prob = dot(value, g_two, ((1,), (1,)))
        delta = jnp.sum(prob * grad_prob, axis=0, keepdims=True)
        grad_score = (prob * (grad_prob - delta)).astype(BF16)
        value_grad += dot(prob_low, g_two, ((1,), (0,)))
        key_grad += dot(grad_score, q_two, ((1,), (0,)))
        out_t = dot(value, prob_low, ((0,), (0,)))
        dq_t = dot(key, grad_score, ((0,), (0,))) * scale
        for i, s in enumerate(spans):
            attn_ref[:, s] = jnp.transpose(out_t[:, i * tok : (i + 1) * tok]).astype(BF16)
            dq_ref[:, s] = jnp.transpose(dq_t[:, i * tok : (i + 1) * tok]).astype(BF16)
    key_grad = key_grad * scale
    own_ref[:, :head] = key_grad[SPAN * tok :, :]
    own_ref[:, head:] = value_grad[SPAN * tok :, :]
    for offset in range(1, SPAN + 1):
        rows = slice((SPAN - offset) * tok, (SPAN - offset + 1) * tok)
        part_refs[offset - 1][:, :head] = key_grad[rows, :].astype(BF16)
        part_refs[offset - 1][:, head:] = value_grad[rows, :].astype(BF16)


def per_device(query, key, value, grad_out, loader_pos, doc_lengths):
    tok, width = query.shape
    head = key.shape[1]
    devices = lax.axis_size("dcp")
    per_peer = tok // devices
    vmem = pl.BlockSpec(memory_space=pltpu.VMEM)
    params = pltpu.CompilerParams(vmem_limit_bytes=48 << 20)
    hbm = pl.BlockSpec(memory_space=pltpu.HBM)
    total = 2 * width + 2 * head * (SPAN + 1)
    paired = devices <= 16 and devices & (devices - 1) == 0
    pieces = devices if paired else 1
    *packed, slots, starts = pl.pallas_call(
        functools.partial(pack_kernel, per_peer, paired),
        out_shape=[jax.ShapeDtypeStruct((tok // pieces, total), BF16)] * pieces
        + [
            jax.ShapeDtypeStruct((tok, LANES), F32),
            jax.ShapeDtypeStruct((8, 2 * tok), jnp.int32),
        ],
        in_specs=[hbm] * 6,
        out_specs=[vmem] * (pieces + 2),
        scratch_shapes=[
            pltpu.VMEM((devices, tok), jnp.int32),
            pltpu.SMEM(doc_lengths.shape, jnp.int32),
            pltpu.VMEM(query.shape, BF16),
            pltpu.VMEM(key.shape, BF16),
            pltpu.VMEM(value.shape, BF16),
            pltpu.VMEM(grad_out.shape, BF16),
            pltpu.SemaphoreType.DMA((6,)),
        ],
        compiler_params=params,
        name="pack",
    )(*[pltpu.with_memory_space_constraint(x, pltpu.HBM) for x in (loader_pos.reshape(devices, tok), doc_lengths, query, key, value, grad_out)])
    if paired:
        for step in range(1, devices):
            partners = [(source, source ^ step) for source in range(devices)]
            packed[step] = lax.ppermute(packed[step], "dcp", partners)
    else:
        packed = [lax.all_to_all(packed[0], "dcp", split_axis=0, concat_axis=0, tiled=True)]
    wide = jax.ShapeDtypeStruct((tok, width), BF16)
    part = jax.ShapeDtypeStruct((tok, 2 * head), BF16)
    attn_out, dquery, summed, *parts = pl.pallas_call(
        functools.partial(attend_kernel, width, head, pieces),
        out_shape=[wide, wide, jax.ShapeDtypeStruct((tok, 2 * head), F32)] + [part] * SPAN,
        in_specs=[vmem] * (2 + pieces),
        out_specs=[vmem] * (3 + SPAN),
        compiler_params=params,
        name="attend",
    )(starts, slots, *packed)
    for offset in (4, 5, 3, 2, 1):
        pairs = [(source, source - offset) for source in range(offset, devices)]
        summed = summed + lax.ppermute(parts[offset - 1], "dcp", pairs).astype(F32)
    return attn_out, dquery, summed[:, :head].astype(BF16), summed[:, head:].astype(BF16)


def solution(mesh):
    rows = P(("rep", "dcp"), None)
    return jax.shard_map(
        per_device,
        mesh=mesh,
        in_specs=(rows, rows, rows, rows, P("rep"), P("rep")),
        out_specs=(rows, rows, rows, rows),
        check_vma=False,
    )
```

```python
import functools
import math

import jax
import jax.numpy as jnp
from jax import lax
from jax.experimental import pallas as pl
from jax.experimental.pallas import tpu as pltpu
from jax.sharding import PartitionSpec as P

SPAN = 5
LANES = 128
NEG = -1e30
F32 = jnp.float32
BF16 = jnp.bfloat16


def dot(a, b, dims):
    return lax.dot_general(a, b, (dims, ((), ())), preferred_element_type=F32)


def rank_of(pos_ref, device):
    tok = pos_ref.shape[1]
    pos_row = pos_ref[pl.ds(device, 1), :]
    pos_col = jnp.transpose(jnp.broadcast_to(pos_row, (tok, tok)))
    return pos_row, jnp.sum((pos_col < pos_row).astype(jnp.int32), axis=0, keepdims=True)


def slots_kernel(per_peer, paired, pos_hbm, len_hbm, _, slot_ref, start_ref, pos_ref, len_ref, sems):
    copies = [
        pltpu.make_async_copy(pos_hbm, pos_ref, sems.at[0]),
        pltpu.make_async_copy(len_hbm, len_ref, sems.at[1]),
    ]
    for copy in copies:
        copy.start()
    devices, tok = pos_ref.shape
    me = lax.axis_index("dcp")
    rows = (SPAN + 1) * per_peer
    window = (me - SPAN) * per_peer + lax.broadcasted_iota(jnp.int32, (rows, tok), 0)
    lane = lax.broadcasted_iota(jnp.int32, (per_peer, LANES), 1)
    copies[0].wait()

    def slots_from(device):
        pos_row, rank = rank_of(pos_ref, device)
        slot = (pos_row % tok).astype(F32)
        column = jnp.sum(jnp.where(rank == window, slot, 0.0), axis=1, keepdims=True)
        slots = jnp.zeros((per_peer, LANES), F32)
        for block in range(SPAN + 1):
            slots = jnp.where(lane == block, column[block * per_peer : (block + 1) * per_peer], slots)
        return slots

    if devices <= 16:
        for source in range(devices):
            device = source ^ me if paired else source
            slot_ref[source * per_peer : (source + 1) * per_peer, :] = slots_from(device)
    else:

        @pl.loop(0, devices)
        def _(source):
            slot_ref[pl.ds(source * per_peer, per_peer), :] = slots_from(source)

    copies[1].wait()
    q_pos = me * tok + lax.broadcasted_iota(jnp.int32, start_ref.shape, 1) % tok
    q_start = jnp.zeros(start_ref.shape, jnp.int32)
    end = jnp.int32(0)
    for doc in range(len_ref.shape[0]):
        end = end + len_ref[doc]
        q_start = jnp.where(q_pos >= end, end, q_start)
    start_ref[...] = q_start


def pack_kernel(
    per_peer, paired, pos_hbm, q_hbm, k_hbm, v_hbm, g_hbm, *rest
):
    out_refs = rest[:-6]
    pos_ref, q_ref, k_ref, v_ref, g_ref, sems = rest[-6:]
    sources = (pos_hbm, k_hbm, v_hbm, q_hbm, g_hbm)
    targets = (pos_ref, k_ref, v_ref, q_ref, g_ref)
    copies = [
        pltpu.make_async_copy(source, target, sems.at[i])
        for i, (source, target) in enumerate(zip(sources, targets))
    ]
    for copy in copies:
        copy.start()
    tok, width = q_ref.shape
    head = k_ref.shape[1]
    me = lax.axis_index("dcp")
    want = lax.broadcasted_iota(jnp.int32, (tok, tok), 0)
    if paired:
        want = ((want // per_peer) ^ me) * per_peer + want % per_peer

    def put(first, rows):
        rows = rows.astype(BF16)
        step = tok // len(out_refs)
        for i, out_ref in enumerate(out_refs):
            out_ref[:, first : first + rows.shape[1]] = rows[i * step : (i + 1) * step]

    copies[0].wait()
    rank = rank_of(pos_ref, me)[1]
    copies[1].wait()
    copies[2].wait()
    for block in range(SPAN + 1):
        perm = (rank == want + (block - SPAN) * per_peer).astype(BF16)
        first = 2 * width + 2 * head * block
        put(first, dot(perm, k_ref[...], ((1,), (0,))))
        put(first + head, dot(perm, v_ref[...], ((1,), (0,))))
    perm = (rank == want).astype(BF16)
    copies[3].wait()
    put(0, dot(perm, q_ref[...], ((1,), (0,))))
    copies[4].wait()
    put(width, dot(perm, g_ref[...], ((1,), (0,))))


def attend_kernel(width, head, pieces, start_ref, slot_ref, *refs):
    in_refs = refs[:pieces]
    key_ref, value_ref, prob_ref, ds_ref, own_ref, *part_refs = refs[pieces:]
    tok = key_ref.shape[0] // (SPAN + 1)
    heads = width // head
    me = lax.axis_index("dcp")
    scale = 1.0 / math.sqrt(head)
    factor = scale * math.log2(math.e)
    base = 2 * width
    slots = slot_ref[...]
    target = lax.broadcasted_iota(jnp.int32, (tok, tok), 1).astype(F32)

    def arrived(first, last):
        return jnp.concatenate([ref[:, first:last] for ref in in_refs], axis=0)

    keys, values = [], []
    place = None
    for block in range(SPAN + 1):
        place = (slots[:, block : block + 1] == target).astype(BF16)
        first = base + 2 * head * block
        both = dot(place, arrived(first, first + 2 * head), ((0,), (0,))).astype(BF16)
        keys.append(both[:, :head])
        values.append(both[:, head:])
    key = jnp.concatenate(keys, axis=0)
    value = jnp.concatenate(values, axis=0)
    key_ref[...] = key
    value_ref[...] = value
    queries = dot(place, arrived(0, width), ((0,), (0,))).astype(BF16)
    grads = dot(place, arrived(width, base), ((0,), (0,))).astype(BF16)

    pairs = 2
    cols = pairs * tok
    window = (SPAN + 1) * tok
    lane = lax.broadcasted_iota(jnp.int32, (1, cols), 1)
    q_pos = me * tok + lane % tok
    q_start = start_ref[:1, :]
    k_pos = (me - SPAN) * tok + lax.broadcasted_iota(jnp.int32, (window, cols), 0)
    allowed = (k_pos >= q_start) & (k_pos <= q_pos)

    key_grad = jnp.zeros((window, head), F32)
    value_grad = jnp.zeros((window, head), F32)
    for first in range(0, heads, pairs):
        spans = [slice(h * head, (h + 1) * head) for h in range(first, first + pairs)]
        q_two = jnp.concatenate([queries[:, s] for s in spans], axis=0)
        g_two = jnp.concatenate([grads[:, s] for s in spans], axis=0)
        scores = jnp.where(allowed, dot(key, q_two, ((1,), (1,))), NEG)
        top = jnp.max(scores, axis=0, keepdims=True)
        weights = jnp.exp2((scores - top) * factor)
        inverse = 1.0 / jnp.sum(weights, axis=0, keepdims=True)
        prob = weights * inverse
        prob_low = prob.astype(BF16)
        grad_prob = dot(value, g_two, ((1,), (1,)))
        delta = jnp.sum(prob * grad_prob, axis=0, keepdims=True)
        grad_score = (prob * (grad_prob - delta)).astype(BF16)
        value_grad += dot(prob_low, g_two, ((1,), (0,)))
        key_grad += dot(grad_score, q_two, ((1,), (0,)))
        prob_ref[:, first * tok : (first + pairs) * tok] = prob_low
        ds_ref[:, first * tok : (first + pairs) * tok] = grad_score
    key_grad = key_grad * scale
    own_ref[:, :head] = key_grad[SPAN * tok :, :]
    own_ref[:, head:] = value_grad[SPAN * tok :, :]
    for offset in range(1, SPAN + 1):
        rows = slice((SPAN - offset) * tok, (SPAN - offset + 1) * tok)
        part_refs[offset - 1][:, :head] = key_grad[rows, :].astype(BF16)
        part_refs[offset - 1][:, head:] = value_grad[rows, :].astype(BF16)


def output_kernel(key_ref, value_ref, prob_ref, ds_ref, attn_ref, dq_ref):
    tok, width = attn_ref.shape
    head = key_ref.shape[1]
    scale = 1.0 / math.sqrt(head)
    pairs = 2
    for first in range(0, width // head, pairs):
        cols = slice(first * tok, (first + pairs) * tok)
        out_t = dot(value_ref[...], prob_ref[:, cols], ((0,), (0,)))
        dq_t = dot(key_ref[...], ds_ref[:, cols], ((0,), (0,))) * scale
        for i in range(pairs):
            s = slice((first + i) * head, (first + i + 1) * head)
            attn_ref[:, s] = jnp.transpose(out_t[:, i * tok : (i + 1) * tok]).astype(BF16)
            dq_ref[:, s] = jnp.transpose(dq_t[:, i * tok : (i + 1) * tok]).astype(BF16)


def per_device(query, key, value, grad_out, loader_pos, doc_lengths):
    tok, width = query.shape
    head = key.shape[1]
    devices = lax.axis_size("dcp")
    per_peer = tok // devices
    vmem = pl.BlockSpec(memory_space=pltpu.VMEM)
    params = pltpu.CompilerParams(vmem_limit_bytes=48 << 20)
    hbm = pl.BlockSpec(memory_space=pltpu.HBM)
    total = 2 * width + 2 * head * (SPAN + 1)
    paired = devices <= 16 and devices & (devices - 1) == 0
    pieces = devices if paired else 1
    positions = pltpu.with_memory_space_constraint(loader_pos.reshape(devices, tok), pltpu.HBM)
    lengths = pltpu.with_memory_space_constraint(doc_lengths, pltpu.HBM)
    sides = [pltpu.with_memory_space_constraint(x, pltpu.HBM) for x in (query, key, value, grad_out)]
    *packed, = pl.pallas_call(
        functools.partial(pack_kernel, per_peer, paired),
        out_shape=[jax.ShapeDtypeStruct((tok // pieces, total), BF16)] * pieces,
        in_specs=[hbm] * 5,
        out_specs=[vmem] * pieces,
        scratch_shapes=[
            pltpu.VMEM((devices, tok), jnp.int32),
            pltpu.VMEM(query.shape, BF16),
            pltpu.VMEM(key.shape, BF16),
            pltpu.VMEM(value.shape, BF16),
            pltpu.VMEM(grad_out.shape, BF16),
            pltpu.SemaphoreType.DMA((5,)),
        ],
        compiler_params=params,
        name="pack",
    )(positions, *sides)
    slots, starts = pl.pallas_call(
        functools.partial(slots_kernel, per_peer, paired),
        out_shape=[
            jax.ShapeDtypeStruct((tok, LANES), F32),
            jax.ShapeDtypeStruct((8, 2 * tok), jnp.int32),
        ],
        in_specs=[hbm, hbm, pl.BlockSpec(memory_space=pl.ANY)],
        out_specs=[vmem] * 2,
        scratch_shapes=[
            pltpu.VMEM((devices, tok), jnp.int32),
            pltpu.SMEM(doc_lengths.shape, jnp.int32),
            pltpu.SemaphoreType.DMA((2,)),
        ],
        compiler_params=params,
        name="slots",
    )(positions, lengths, packed[0])
    if paired:
        for step in range(1, devices):
            partners = [(source, source ^ step) for source in range(devices)]
            packed[step] = lax.ppermute(packed[step], "dcp", partners)
    else:
        packed = [lax.all_to_all(packed[0], "dcp", split_axis=0, concat_axis=0, tiled=True)]
    wide = jax.ShapeDtypeStruct((tok, width), BF16)
    rows = (SPAN + 1) * tok
    seen = jax.ShapeDtypeStruct((rows, head), BF16)
    square = jax.ShapeDtypeStruct((rows, tok * width // head), BF16)
    part = jax.ShapeDtypeStruct((tok, 2 * head), BF16)
    keys, values, probs, grad_scores, summed, *parts = pl.pallas_call(
        functools.partial(attend_kernel, width, head, pieces),
        out_shape=[seen, seen, square, square, jax.ShapeDtypeStruct((tok, 2 * head), F32)] + [part] * SPAN,
        in_specs=[vmem] * (2 + pieces),
        out_specs=[vmem] * (5 + SPAN),
        compiler_params=params,
        name="attend",
    )(starts, slots, *packed)
    attn_out, dquery = pl.pallas_call(
        output_kernel,
        out_shape=[wide, wide],
        in_specs=[vmem] * 4,
        out_specs=[vmem] * 2,
        compiler_params=params,
        name="outputs",
    )(keys, values, probs, grad_scores)
    for offset in range(SPAN, 0, -1):
        pairs = [(source, source - offset) for source in range(offset, devices)]
        summed = summed + lax.ppermute(parts[offset - 1], "dcp", pairs).astype(F32)
    return attn_out, dquery, summed[:, :head].astype(BF16), summed[:, head:].astype(BF16)


def solution(mesh):
    rows = P(("rep", "dcp"), None)
    return jax.shard_map(
        per_device,
        mesh=mesh,
        in_specs=(rows, rows, rows, rows, P("rep"), P("rep")),
        out_specs=(rows, rows, rows, rows),
        check_vma=False,
    )
```

```python
import functools
import math

import jax
import jax.numpy as jnp
from jax import lax
from jax.experimental import pallas as pl
from jax.experimental.pallas import tpu as pltpu
from jax.sharding import PartitionSpec as P

SPAN = 5
LANES = 128
NEG = -1e30
F32 = jnp.float32
BF16 = jnp.bfloat16


def dot(a, b, dims):
    return lax.dot_general(a, b, (dims, ((), ())), preferred_element_type=F32)


def rank_of(pos_ref, device):
    tok = pos_ref.shape[1]
    pos_row = pos_ref[pl.ds(device, 1), :]
    pos_col = jnp.transpose(jnp.broadcast_to(pos_row, (tok, tok)))
    return pos_row, jnp.sum((pos_col < pos_row).astype(jnp.int32), axis=0, keepdims=True)


def slots_kernel(per_peer, paired, pos_hbm, len_hbm, _, slot_ref, start_ref, pos_ref, len_ref, sems):
    copies = [
        pltpu.make_async_copy(pos_hbm, pos_ref, sems.at[0]),
        pltpu.make_async_copy(len_hbm, len_ref, sems.at[1]),
    ]
    for copy in copies:
        copy.start()
    devices, tok = pos_ref.shape
    me = lax.axis_index("dcp")
    rows = (SPAN + 1) * per_peer
    window = (me - SPAN) * per_peer + lax.broadcasted_iota(jnp.int32, (rows, tok), 0)
    lane = lax.broadcasted_iota(jnp.int32, (per_peer, LANES), 1)
    copies[0].wait()

    def slots_from(device):
        pos_row, rank = rank_of(pos_ref, device)
        slot = (pos_row % tok).astype(F32)
        column = jnp.sum(jnp.where(rank == window, slot, 0.0), axis=1, keepdims=True)
        slots = jnp.zeros((per_peer, LANES), F32)
        for block in range(SPAN + 1):
            slots = jnp.where(lane == block, column[block * per_peer : (block + 1) * per_peer], slots)
        return slots

    if devices <= 16:
        for source in range(devices):
            device = source ^ me if paired else source
            slot_ref[source * per_peer : (source + 1) * per_peer, :] = slots_from(device)
    else:

        @pl.loop(0, devices)
        def _(source):
            slot_ref[pl.ds(source * per_peer, per_peer), :] = slots_from(source)

    copies[1].wait()
    q_pos = me * tok + lax.broadcasted_iota(jnp.int32, start_ref.shape, 1) % tok
    q_start = jnp.zeros(start_ref.shape, jnp.int32)
    end = jnp.int32(0)
    for doc in range(len_ref.shape[0]):
        end = end + len_ref[doc]
        q_start = jnp.where(q_pos >= end, end, q_start)
    start_ref[...] = q_start


def order_kernel(pos_hbm, k_hbm, v_hbm, out_ref, pos_ref, k_ref, v_ref, sems):
    sources, targets = (pos_hbm, k_hbm, v_hbm), (pos_ref, k_ref, v_ref)
    copies = [
        pltpu.make_async_copy(source, target, sems.at[i])
        for i, (source, target) in enumerate(zip(sources, targets))
    ]
    for copy in copies:
        copy.start()
    tok, head = k_ref.shape
    copies[0].wait()
    rank = rank_of(pos_ref, lax.axis_index("dcp"))[1]
    perm = (rank == lax.broadcasted_iota(jnp.int32, (tok, tok), 0)).astype(BF16)
    copies[1].wait()
    out_ref[:, :head] = dot(perm, k_ref[...], ((1,), (0,))).astype(BF16)
    copies[2].wait()
    out_ref[:, head:] = dot(perm, v_ref[...], ((1,), (0,))).astype(BF16)


def pack_kernel(per_peer, paired, pos_hbm, q_hbm, g_hbm, both_ref, *rest):
    out_refs = rest[:-4]
    pos_ref, q_ref, g_ref, sems = rest[-4:]
    sources, targets = (pos_hbm, q_hbm, g_hbm), (pos_ref, q_ref, g_ref)
    copies = [
        pltpu.make_async_copy(source, target, sems.at[i])
        for i, (source, target) in enumerate(zip(sources, targets))
    ]
    for copy in copies:
        copy.start()
    tok, width = q_ref.shape
    two = both_ref.shape[1]
    me = lax.axis_index("dcp")
    step = tok // len(out_refs)
    near = max(1, len(out_refs) // 2)
    want = lax.broadcasted_iota(jnp.int32, (tok, tok), 0)
    lane = lax.broadcasted_iota(jnp.int32, (tok, tok), 1)
    if paired:
        want = ((want // per_peer) ^ me) * per_peer + want % per_peer

    def put(first, rows):
        rows = rows.astype(BF16)
        for i in range(rows.shape[0] // step):
            out_refs[i][:, first : first + rows.shape[1]] = rows[i * step : (i + 1) * step]

    both = both_ref[...]
    for block in range(SPAN + 1):
        perm = (lane == want + (block - SPAN) * per_peer)[: near * step].astype(BF16)
        put(2 * width + two * block, dot(perm, both, ((1,), (0,))))
    copies[0].wait()
    rank = rank_of(pos_ref, me)[1]
    perm = (rank == want).astype(BF16)
    copies[1].wait()
    put(0, dot(perm, q_ref[...], ((1,), (0,))))
    copies[2].wait()
    put(width, dot(perm, g_ref[...], ((1,), (0,))))


def attend_kernel(width, head, pieces, start_ref, slot_ref, *refs):
    near = max(1, pieces // 2)
    count = pieces + (near if pieces > 1 else 0)
    in_refs = refs[:pieces]
    key_ref, value_ref, prob_ref, ds_ref, own_ref, *part_refs = refs[count:]
    tok = key_ref.shape[0] // (SPAN + 1)
    heads = width // head
    me = lax.axis_index("dcp")
    scale = 1.0 / math.sqrt(head)
    factor = scale * math.log2(math.e)
    base = 2 * width
    slots = slot_ref[...]
    target = lax.broadcasted_iota(jnp.int32, (tok, tok), 1).astype(F32)

    def arrived(first, last):
        return jnp.concatenate([ref[:, first:last] for ref in in_refs], axis=0)

    def window(block):
        first = base + 2 * head * block
        parts = [ref[:, first : first + 2 * head] for ref in in_refs[:near]]
        step = tok // pieces
        rows = pl.ds(pl.multiple_of(step * jnp.maximum(me - SPAN + block, 0), step), step)
        parts += [ref[rows, :] for ref in refs[pieces:count]]
        return jnp.concatenate(parts, axis=0)

    keys, values = [], []
    place = None
    for block in range(SPAN + 1):
        place = (slots[:, block : block + 1] == target).astype(BF16)
        both = dot(place, window(block), ((0,), (0,))).astype(BF16)
        keys.append(both[:, :head])
        values.append(both[:, head:])
    key = jnp.concatenate(keys, axis=0)
    value = jnp.concatenate(values, axis=0)
    key_ref[...] = key
    value_ref[...] = value
    queries = dot(place, arrived(0, width), ((0,), (0,))).astype(BF16)
    grads = dot(place, arrived(width, base), ((0,), (0,))).astype(BF16)

    pairs = 2
    cols = pairs * tok
    window = (SPAN + 1) * tok
    lane = lax.broadcasted_iota(jnp.int32, (1, cols), 1)
    q_pos = me * tok + lane % tok
    q_start = start_ref[:1, :]
    k_pos = (me - SPAN) * tok + lax.broadcasted_iota(jnp.int32, (window, cols), 0)
    allowed = (k_pos >= q_start) & (k_pos <= q_pos)

    key_grad = jnp.zeros((window, head), F32)
    value_grad = jnp.zeros((window, head), F32)
    for first in range(0, heads, pairs):
        spans = [slice(h * head, (h + 1) * head) for h in range(first, first + pairs)]
        q_two = jnp.concatenate([queries[:, s] for s in spans], axis=0)
        g_two = jnp.concatenate([grads[:, s] for s in spans], axis=0)
        scores = jnp.where(allowed, dot(key, q_two, ((1,), (1,))), NEG)
        top = jnp.max(scores, axis=0, keepdims=True)
        weights = jnp.exp2((scores - top) * factor)
        inverse = 1.0 / jnp.sum(weights, axis=0, keepdims=True)
        prob = weights * inverse
        prob_low = prob.astype(BF16)
        grad_prob = dot(value, g_two, ((1,), (1,)))
        delta = jnp.sum(prob * grad_prob, axis=0, keepdims=True)
        grad_score = (prob * (grad_prob - delta)).astype(BF16)
        value_grad += dot(prob_low, g_two, ((1,), (0,)))
        key_grad += dot(grad_score, q_two, ((1,), (0,)))
        prob_ref[:, first * tok : (first + pairs) * tok] = prob_low
        ds_ref[:, first * tok : (first + pairs) * tok] = grad_score
    key_grad = key_grad * scale
    own_ref[:, :head] = key_grad[SPAN * tok :, :]
    own_ref[:, head:] = value_grad[SPAN * tok :, :]
    for offset in range(1, SPAN + 1):
        rows = slice((SPAN - offset) * tok, (SPAN - offset + 1) * tok)
        part_refs[offset - 1][:, :head] = key_grad[rows, :].astype(BF16)
        part_refs[offset - 1][:, head:] = value_grad[rows, :].astype(BF16)


def output_kernel(key_ref, value_ref, prob_ref, ds_ref, attn_ref, dq_ref):
    tok, width = attn_ref.shape
    head = key_ref.shape[1]
    scale = 1.0 / math.sqrt(head)
    pairs = 2
    for first in range(0, width // head, pairs):
        cols = slice(first * tok, (first + pairs) * tok)
        out_t = dot(value_ref[...], prob_ref[:, cols], ((0,), (0,)))
        dq_t = dot(key_ref[...], ds_ref[:, cols], ((0,), (0,))) * scale
        for i in range(pairs):
            s = slice((first + i) * head, (first + i + 1) * head)
            attn_ref[:, s] = jnp.transpose(out_t[:, i * tok : (i + 1) * tok]).astype(BF16)
            dq_ref[:, s] = jnp.transpose(dq_t[:, i * tok : (i + 1) * tok]).astype(BF16)


def per_device(query, key, value, grad_out, loader_pos, doc_lengths):
    tok, width = query.shape
    head = key.shape[1]
    devices = lax.axis_size("dcp")
    per_peer = tok // devices
    vmem = pl.BlockSpec(memory_space=pltpu.VMEM)
    params = pltpu.CompilerParams(vmem_limit_bytes=48 << 20)
    hbm = pl.BlockSpec(memory_space=pltpu.HBM)
    base = 2 * width
    total = base + 2 * head * (SPAN + 1)
    paired = devices <= 16 and devices & (devices - 1) == 0
    pieces = devices if paired else 1
    positions = pltpu.with_memory_space_constraint(loader_pos.reshape(devices, tok), pltpu.HBM)
    lengths = pltpu.with_memory_space_constraint(doc_lengths, pltpu.HBM)
    sides = [pltpu.with_memory_space_constraint(x, pltpu.HBM) for x in (query, key, value, grad_out)]
    near = devices // 2
    widths = [total] * near + [base] * near if paired else [total]
    ordered = pl.pallas_call(
        order_kernel,
        out_shape=jax.ShapeDtypeStruct((tok, 2 * head), BF16),
        in_specs=[hbm] * 3,
        out_specs=vmem,
        scratch_shapes=[
            pltpu.VMEM((devices, tok), jnp.int32),
            pltpu.VMEM(key.shape, BF16),
            pltpu.VMEM(value.shape, BF16),
            pltpu.SemaphoreType.DMA((3,)),
        ],
        compiler_params=params,
        name="order",
    )(positions, sides[1], sides[2])

    def swapped(rows, step):
        return lax.ppermute(rows, "dcp", [(d, d ^ step) for d in range(devices)])

    across = [swapped(ordered, near)] if paired else []
    *packed, = pl.pallas_call(
        functools.partial(pack_kernel, per_peer, paired),
        out_shape=[jax.ShapeDtypeStruct((tok // pieces, cols), BF16) for cols in widths],
        in_specs=[hbm, hbm, hbm, vmem],
        out_specs=[vmem] * pieces,
        scratch_shapes=[
            pltpu.VMEM((devices, tok), jnp.int32),
            pltpu.VMEM(query.shape, BF16),
            pltpu.VMEM(grad_out.shape, BF16),
            pltpu.SemaphoreType.DMA((3,)),
        ],
        compiler_params=params,
        cost_estimate=pl.CostEstimate(flops=1 << 27, bytes_accessed=3 << 20, transcendentals=0),
        name="pack",
    )(positions, sides[0], sides[3], ordered)
    slots, starts = pl.pallas_call(
        functools.partial(slots_kernel, per_peer, paired),
        out_shape=[
            jax.ShapeDtypeStruct((tok, LANES), F32),
            jax.ShapeDtypeStruct((8, 2 * tok), jnp.int32),
        ],
        in_specs=[hbm, hbm, pl.BlockSpec(memory_space=pl.ANY)],
        out_specs=[vmem] * 2,
        scratch_shapes=[
            pltpu.VMEM((devices, tok), jnp.int32),
            pltpu.SMEM(doc_lengths.shape, jnp.int32),
            pltpu.SemaphoreType.DMA((2,)),
        ],
        compiler_params=params,
        name="slots",
    )(positions, lengths, packed[0])
    if paired:
        for step in range(near, devices):
            packed[step] = swapped(packed[step], step)
        across[0], *packed[1:near] = lax.optimization_barrier((across[0], *packed[1:near]))
        across += [swapped(across[0], step) for step in range(1, near)]
        for step in range(1, near):
            packed[step] = swapped(packed[step], step)
    else:
        packed = [lax.all_to_all(packed[0], "dcp", split_axis=0, concat_axis=0, tiled=True)]
    wide = jax.ShapeDtypeStruct((tok, width), BF16)
    rows = (SPAN + 1) * tok
    seen = jax.ShapeDtypeStruct((rows, head), BF16)
    square = jax.ShapeDtypeStruct((rows, tok * width // head), BF16)
    part = jax.ShapeDtypeStruct((tok, 2 * head), BF16)
    keys, values, probs, grad_scores, summed, *parts = pl.pallas_call(
        functools.partial(attend_kernel, width, head, pieces),
        out_shape=[seen, seen, square, square, jax.ShapeDtypeStruct((tok, 2 * head), F32)] + [part] * SPAN,
        in_specs=[vmem] * (2 + pieces + len(across)),
        out_specs=[vmem] * (5 + SPAN),
        compiler_params=params,
        name="attend",
    )(starts, slots, *packed, *across)
    attn_out, dquery = pl.pallas_call(
        output_kernel,
        out_shape=[wide, wide],
        in_specs=[vmem] * 4,
        out_specs=[vmem] * 2,
        compiler_params=params,
        name="outputs",
    )(keys, values, probs, grad_scores)
    for offset in range(SPAN, 0, -1):
        pairs = [(source, source - offset) for source in range(offset, devices)]
        summed = summed + lax.ppermute(parts[offset - 1], "dcp", pairs).astype(F32)
    return attn_out, dquery, summed[:, :head].astype(BF16), summed[:, head:].astype(BF16)


def solution(mesh):
    rows = P(("rep", "dcp"), None)
    return jax.shard_map(
        per_device,
        mesh=mesh,
        in_specs=(rows, rows, rows, rows, P("rep"), P("rep")),
        out_specs=(rows, rows, rows, rows),
        check_vma=False,
    )
```

```python
import functools
import math

import jax
import jax.numpy as jnp
from jax import lax
from jax.experimental import pallas as pl
from jax.experimental.pallas import tpu as pltpu
from jax.sharding import PartitionSpec as P

SPAN = 5
LANES = 128
NEG = -1e30
F32 = jnp.float32
BF16 = jnp.bfloat16


def dot(a, b, dims):
    return lax.dot_general(a, b, (dims, ((), ())), preferred_element_type=F32)


def rank_of(pos_ref, device):
    tok = pos_ref.shape[1]
    pos_row = pos_ref[pl.ds(device, 1), :]
    pos_col = jnp.transpose(jnp.broadcast_to(pos_row, (tok, tok)))
    return pos_row, jnp.sum((pos_col < pos_row).astype(jnp.int32), axis=0, keepdims=True)


def slots_kernel(per_peer, paired, pos_hbm, len_hbm, _, slot_ref, start_ref, pos_ref, len_ref, sems):
    copies = [
        pltpu.make_async_copy(pos_hbm, pos_ref, sems.at[0]),
        pltpu.make_async_copy(len_hbm, len_ref, sems.at[1]),
    ]
    for copy in copies:
        copy.start()
    devices, tok = pos_ref.shape
    me = lax.axis_index("dcp")
    rows = (SPAN + 1) * per_peer
    window = (me - SPAN) * per_peer + lax.broadcasted_iota(jnp.int32, (rows, tok), 0)
    lane = lax.broadcasted_iota(jnp.int32, (per_peer, LANES), 1)
    copies[0].wait()

    def slots_from(device):
        pos_row, rank = rank_of(pos_ref, device)
        slot = (pos_row % tok).astype(F32)
        column = jnp.sum(jnp.where(rank == window, slot, 0.0), axis=1, keepdims=True)
        slots = jnp.zeros((per_peer, LANES), F32)
        for block in range(SPAN + 1):
            slots = jnp.where(lane == block, column[block * per_peer : (block + 1) * per_peer], slots)
        return slots

    if devices <= 16:
        for source in range(devices):
            device = source ^ me if paired else source
            slot_ref[source * per_peer : (source + 1) * per_peer, :] = slots_from(device)
    else:

        @pl.loop(0, devices)
        def _(source):
            slot_ref[pl.ds(source * per_peer, per_peer), :] = slots_from(source)

    copies[1].wait()
    q_pos = me * tok + lax.broadcasted_iota(jnp.int32, start_ref.shape, 1) % tok
    q_start = jnp.zeros(start_ref.shape, jnp.int32)
    end = jnp.int32(0)
    for doc in range(len_ref.shape[0]):
        end = end + len_ref[doc]
        q_start = jnp.where(q_pos >= end, end, q_start)
    start_ref[...] = q_start


def group_rows(per_peer, paired, tok):
    want = lax.broadcasted_iota(jnp.int32, (tok, tok), 0)
    if paired:
        want = ((want // per_peer) ^ lax.axis_index("dcp")) * per_peer + want % per_peer
    return want


def pack_kernel(per_peer, paired, pos_hbm, k_hbm, v_hbm, q_hbm, g_hbm, *rest):
    ordered_ref, *out_refs = rest[:-6]
    *targets, sems = rest[-6:]
    copies = [
        pltpu.make_async_copy(source, target, sems.at[i])
        for i, (source, target) in enumerate(zip((pos_hbm, k_hbm, v_hbm, q_hbm, g_hbm), targets))
    ]
    for copy in copies:
        copy.start()
    pos_ref, k_ref, v_ref, q_ref, g_ref = targets
    tok, width = q_ref.shape
    head = k_ref.shape[1]
    step = tok // len(out_refs)
    copies[0].wait()
    rank = rank_of(pos_ref, lax.axis_index("dcp"))[1]
    perm = (rank == lax.broadcasted_iota(jnp.int32, (tok, tok), 0)).astype(BF16)
    for side, ref in enumerate((k_ref, v_ref)):
        copies[1 + side].wait()
        ordered_ref[:, side * head : (side + 1) * head] = dot(perm, ref[...], ((1,), (0,))).astype(BF16)
    perm = (rank == group_rows(per_peer, paired, tok)).astype(BF16)
    for side, ref in enumerate((q_ref, g_ref)):
        copies[3 + side].wait()
        rows = dot(perm, ref[...], ((1,), (0,))).astype(BF16)
        for i, out_ref in enumerate(out_refs):
            out_ref[:, side * width : (side + 1) * width] = rows[i * step : (i + 1) * step]


def near_kernel(per_peer, paired, pairs, *refs):
    pair_refs, refs = refs[:pairs], refs[pairs:]
    near = len(refs) // 2
    step, base = refs[0].shape
    tok, two = pair_refs[0].shape
    want = group_rows(per_peer, paired, tok)[: near * step]
    lane = lax.broadcasted_iota(jnp.int32, want.shape, 1)
    for i in range(near):
        refs[near + i][:, :base] = refs[i][...]
    for block in range(SPAN + 1):
        perm = (lane == want + (block - SPAN) * per_peer).astype(BF16)
        for side, ref in enumerate(pair_refs):
            rows = dot(perm, ref[...], ((1,), (0,))).astype(BF16)
            first = base + two * (side * (SPAN + 1) + block)
            for i in range(near):
                refs[near + i][:, first : first + two] = rows[i * step : (i + 1) * step]


def far_kernel(slot_ref, *refs):
    *in_refs, out_ref = refs
    rows = jnp.concatenate([ref[...] for ref in in_refs], axis=0)
    slots = slot_ref[slot_ref.shape[0] - rows.shape[0] :, SPAN : SPAN + 1]
    target = lax.broadcasted_iota(jnp.int32, (rows.shape[0], out_ref.shape[0]), 1).astype(F32)
    out_ref[...] = dot((slots == target).astype(BF16), rows, ((0,), (0,))).astype(BF16)


def attend_kernel(width, head, pieces, start_ref, slot_ref, *refs):
    near = max(1, pieces // 2)
    in_refs = refs[:near]
    refs = refs[near:]
    if pieces > near:
        far_ref, *refs = refs
    key_ref, value_ref, prob_ref, ds_ref, own_ref, *part_refs = refs
    tok = key_ref.shape[0] // (SPAN + 1)
    heads = width // head
    me = lax.axis_index("dcp")
    scale = 1.0 / math.sqrt(head)
    factor = scale * math.log2(math.e)
    base = 2 * width
    slots = slot_ref[...]
    target = lax.broadcasted_iota(jnp.int32, (tok, tok), 1).astype(F32)

    def arrived(first, last):
        return jnp.concatenate([ref[:, first:last] for ref in in_refs], axis=0)

    def window(block):
        parts = []
        for side in range(pieces // near):
            first = base + 2 * head * (side * (SPAN + 1) + block)
            parts += [ref[:, first : first + 2 * head] for ref in in_refs[:near]]
        return jnp.concatenate(parts, axis=0)

    keys, values = [], []
    place = None
    for block in range(SPAN + 1):
        place = (slots[:, block : block + 1] == target).astype(BF16)
        both = dot(place, window(block), ((0,), (0,))).astype(BF16)
        keys.append(both[:, :head])
        values.append(both[:, head:])
    key = jnp.concatenate(keys, axis=0)
    value = jnp.concatenate(values, axis=0)
    key_ref[...] = key
    value_ref[...] = value
    place = place[: tok // pieces * near]

    def placed(first, last):
        rows = dot(place, arrived(first, last), ((0,), (0,)))
        if pieces > near:
            rows = rows + far_ref[:, first:last].astype(F32)
        return rows.astype(BF16)

    queries = placed(0, width)
    grads = placed(width, base)

    pairs = 2
    cols = pairs * tok
    window = (SPAN + 1) * tok
    lane = lax.broadcasted_iota(jnp.int32, (1, cols), 1)
    q_pos = me * tok + lane % tok
    q_start = start_ref[:1, :]
    k_pos = (me - SPAN) * tok + lax.broadcasted_iota(jnp.int32, (window, cols), 0)
    allowed = (k_pos >= q_start) & (k_pos <= q_pos)

    key_grad = jnp.zeros((window, head), F32)
    value_grad = jnp.zeros((window, head), F32)
    for first in range(0, heads, pairs):
        spans = [slice(h * head, (h + 1) * head) for h in range(first, first + pairs)]
        q_two = jnp.concatenate([queries[:, s] for s in spans], axis=0)
        g_two = jnp.concatenate([grads[:, s] for s in spans], axis=0)
        scores = jnp.where(allowed, dot(key, q_two, ((1,), (1,))), NEG)
        top = jnp.max(scores, axis=0, keepdims=True)
        weights = jnp.exp2((scores - top) * factor)
        inverse = 1.0 / jnp.sum(weights, axis=0, keepdims=True)
        prob = weights * inverse
        prob_low = prob.astype(BF16)
        grad_prob = dot(value, g_two, ((1,), (1,)))
        delta = jnp.sum(prob * grad_prob, axis=0, keepdims=True)
        grad_score = (prob * (grad_prob - delta)).astype(BF16)
        value_grad += dot(prob_low, g_two, ((1,), (0,)))
        key_grad += dot(grad_score, q_two, ((1,), (0,)))
        prob_ref[:, first * tok : (first + pairs) * tok] = prob_low
        ds_ref[:, first * tok : (first + pairs) * tok] = grad_score
    key_grad = key_grad * scale
    own_ref[:, :head] = key_grad[SPAN * tok :, :]
    own_ref[:, head:] = value_grad[SPAN * tok :, :]
    for offset in range(1, SPAN + 1):
        rows = slice((SPAN - offset) * tok, (SPAN - offset + 1) * tok)
        part_refs[offset - 1][:, :head] = key_grad[rows, :].astype(BF16)
        part_refs[offset - 1][:, head:] = value_grad[rows, :].astype(BF16)


def output_kernel(key_ref, value_ref, prob_ref, ds_ref, attn_ref, dq_ref):
    tok, width = attn_ref.shape
    head = key_ref.shape[1]
    scale = 1.0 / math.sqrt(head)
    pairs = 2
    for first in range(0, width // head, pairs):
        cols = slice(first * tok, (first + pairs) * tok)
        out_t = dot(value_ref[...], prob_ref[:, cols], ((0,), (0,)))
        dq_t = dot(key_ref[...], ds_ref[:, cols], ((0,), (0,))) * scale
        for i in range(pairs):
            s = slice((first + i) * head, (first + i + 1) * head)
            attn_ref[:, s] = jnp.transpose(out_t[:, i * tok : (i + 1) * tok]).astype(BF16)
            dq_ref[:, s] = jnp.transpose(dq_t[:, i * tok : (i + 1) * tok]).astype(BF16)


def per_device(query, key, value, grad_out, loader_pos, doc_lengths):
    tok, width = query.shape
    head = key.shape[1]
    devices = lax.axis_size("dcp")
    per_peer = tok // devices
    vmem = pl.BlockSpec(memory_space=pltpu.VMEM)
    params = pltpu.CompilerParams(vmem_limit_bytes=48 << 20)
    hbm = pl.BlockSpec(memory_space=pltpu.HBM)
    base = 2 * width
    paired = devices <= 16 and devices & (devices - 1) == 0
    pieces = devices if paired else 1
    positions = pltpu.with_memory_space_constraint(loader_pos.reshape(devices, tok), pltpu.HBM)
    lengths = pltpu.with_memory_space_constraint(doc_lengths, pltpu.HBM)
    sides = [pltpu.with_memory_space_constraint(x, pltpu.HBM) for x in (query, key, value, grad_out)]
    near = max(1, pieces // 2)
    def swapped(rows, step):
        return lax.ppermute(rows, "dcp", [(d, d ^ step) for d in range(devices)])

    ordered, *packed = pl.pallas_call(
        functools.partial(pack_kernel, per_peer, paired),
        out_shape=[jax.ShapeDtypeStruct((tok, 2 * head), BF16)]
        + [jax.ShapeDtypeStruct((tok // pieces, base), BF16)] * pieces,
        in_specs=[hbm] * 5,
        out_specs=[vmem] * (1 + pieces),
        scratch_shapes=[
            pltpu.VMEM((devices, tok), jnp.int32),
            pltpu.VMEM(key.shape, BF16),
            pltpu.VMEM(value.shape, BF16),
            pltpu.VMEM(query.shape, BF16),
            pltpu.VMEM(grad_out.shape, BF16),
            pltpu.SemaphoreType.DMA((5,)),
        ],
        compiler_params=params,
        name="pack",
    )(positions, sides[1], sides[2], sides[0], sides[3])
    held = [ordered, swapped(ordered, near)] if paired else [ordered]
    for step in range(near, pieces if paired else 0):
        packed[step] = swapped(packed[step], step)
    cols = base + 2 * head * (SPAN + 1) * len(held)
    packed[:near] = pl.pallas_call(
        functools.partial(near_kernel, per_peer, paired, len(held)),
        out_shape=[jax.ShapeDtypeStruct((tok // pieces, cols), BF16)] * near,
        in_specs=[vmem] * (len(held) + near),
        out_specs=[vmem] * near,
        compiler_params=params,
        name="near",
    )(*held, *packed[:near])
    if paired:
        for step in range(1, near):
            packed[step] = swapped(packed[step], step)
    else:
        packed = [lax.all_to_all(packed[0], "dcp", split_axis=0, concat_axis=0, tiled=True)]
    slots, starts = pl.pallas_call(
        functools.partial(slots_kernel, per_peer, paired),
        out_shape=[
            jax.ShapeDtypeStruct((tok, LANES), F32),
            jax.ShapeDtypeStruct((8, 2 * tok), jnp.int32),
        ],
        in_specs=[hbm, hbm, pl.BlockSpec(memory_space=pl.ANY)],
        out_specs=[vmem] * 2,
        scratch_shapes=[
            pltpu.VMEM((devices, tok), jnp.int32),
            pltpu.SMEM(doc_lengths.shape, jnp.int32),
            pltpu.SemaphoreType.DMA((2,)),
        ],
        compiler_params=params,
        name="slots",
    )(positions, lengths, packed[0])
    wide = jax.ShapeDtypeStruct((tok, width), BF16)
    if paired:
        far = pl.pallas_call(
            far_kernel,
            out_shape=jax.ShapeDtypeStruct((tok, base), BF16),
            in_specs=[vmem] * (1 + pieces - near),
            out_specs=vmem,
            compiler_params=params,
            cost_estimate=pl.CostEstimate(flops=1 << 33, bytes_accessed=1 << 20, transcendentals=0),
            name="far",
        )(slots, *packed[near:])
        packed[near:] = [far]
    rows = (SPAN + 1) * tok
    seen = jax.ShapeDtypeStruct((rows, head), BF16)
    square = jax.ShapeDtypeStruct((rows, tok * width // head), BF16)
    part = jax.ShapeDtypeStruct((tok, 2 * head), BF16)
    keys, values, probs, grad_scores, summed, *parts = pl.pallas_call(
        functools.partial(attend_kernel, width, head, pieces),
        out_shape=[seen, seen, square, square, jax.ShapeDtypeStruct((tok, 2 * head), F32)] + [part] * SPAN,
        in_specs=[vmem] * (2 + len(packed)),
        out_specs=[vmem] * (5 + SPAN),
        compiler_params=params,
        name="attend",
    )(starts, slots, *packed)
    attn_out, dquery = pl.pallas_call(
        output_kernel,
        out_shape=[wide, wide],
        in_specs=[vmem] * 4,
        out_specs=[vmem] * 2,
        compiler_params=params,
        name="outputs",
    )(keys, values, probs, grad_scores)
    for offset in range(SPAN, 0, -1):
        pairs = [(source, source - offset) for source in range(offset, devices)]
        summed = summed + lax.ppermute(parts[offset - 1], "dcp", pairs).astype(F32)
    return attn_out, dquery, summed[:, :head].astype(BF16), summed[:, head:].astype(BF16)


def solution(mesh):
    rows = P(("rep", "dcp"), None)
    return jax.shard_map(
        per_device,
        mesh=mesh,
        in_specs=(rows, rows, rows, rows, P("rep"), P("rep")),
        out_specs=(rows, rows, rows, rows),
        check_vma=False,
    )
```

```python
import functools
import math

import jax
import jax.numpy as jnp
from jax import lax
from jax.experimental import pallas as pl
from jax.experimental.pallas import tpu as pltpu
from jax.sharding import PartitionSpec as P

SPAN = 5
LANES = 128
NEG = -1e30
F32 = jnp.float32
BF16 = jnp.bfloat16


def dot(a, b, dims):
    return lax.dot_general(a, b, (dims, ((), ())), preferred_element_type=F32)


def rank_of(pos_ref, device):
    tok = pos_ref.shape[1]
    pos_row = pos_ref[pl.ds(device, 1), :]
    pos_col = jnp.transpose(jnp.broadcast_to(pos_row, (tok, tok)))
    return pos_row, jnp.sum((pos_col < pos_row).astype(jnp.int32), axis=0, keepdims=True)


def slots_kernel(per_peer, paired, pos_hbm, len_hbm, _, place_ref, mask_ref, pos_ref, len_ref, slot_ref, sems):
    copies = [
        pltpu.make_async_copy(pos_hbm, pos_ref, sems.at[0]),
        pltpu.make_async_copy(len_hbm, len_ref, sems.at[1]),
    ]
    for copy in copies:
        copy.start()
    devices, tok = pos_ref.shape
    me = lax.axis_index("dcp")
    rows = (SPAN + 1) * per_peer
    window = (me - SPAN) * per_peer + lax.broadcasted_iota(jnp.int32, (rows, tok), 0)
    lane = lax.broadcasted_iota(jnp.int32, (per_peer, LANES), 1)
    copies[0].wait()

    def slots_from(device):
        pos_row, rank = rank_of(pos_ref, device)
        slot = (pos_row % tok).astype(F32)
        column = jnp.sum(jnp.where(rank == window, slot, 0.0), axis=1, keepdims=True)
        slots = jnp.zeros((per_peer, LANES), F32)
        for block in range(SPAN + 1):
            slots = jnp.where(lane == block, column[block * per_peer : (block + 1) * per_peer], slots)
        return slots

    if devices <= 16:
        for source in range(devices):
            device = source ^ me if paired else source
            slot_ref[source * per_peer : (source + 1) * per_peer, :] = slots_from(device)
    else:

        @pl.loop(0, devices)
        def _(source):
            slot_ref[pl.ds(source * per_peer, per_peer), :] = slots_from(source)

    slot = lax.broadcasted_iota(jnp.int32, (tok, tok), 0).astype(F32)
    arrived = jnp.transpose(slot_ref[...])
    for block in range(SPAN + 1):
        rows = slice(block * tok, (block + 1) * tok)
        place_ref[rows, :] = (arrived[block : block + 1, :] == slot).astype(BF16)

    copies[1].wait()
    q_pos = me * tok + lax.broadcasted_iota(jnp.int32, (1, tok), 1)
    q_start = jnp.zeros((1, tok), jnp.int32)
    end = jnp.int32(0)
    for doc in range(len_ref.shape[0]):
        end = end + len_ref[doc]
        q_start = jnp.where(q_pos >= end, end, q_start)
    k_pos = (me - SPAN) * tok + lax.broadcasted_iota(jnp.int32, mask_ref.shape, 0)
    mask_ref[...] = jnp.where((k_pos >= q_start) & (k_pos <= q_pos), 0.0, NEG)


def group_rows(per_peer, paired, tok):
    want = lax.broadcasted_iota(jnp.int32, (tok, tok), 0)
    if paired:
        want = ((want // per_peer) ^ lax.axis_index("dcp")) * per_peer + want % per_peer
    return want


def pack_kernel(per_peer, paired, pos_hbm, k_hbm, v_hbm, q_hbm, g_hbm, *rest):
    ordered_ref, *out_refs = rest[:-6]
    *targets, sems = rest[-6:]
    copies = [
        pltpu.make_async_copy(source, target, sems.at[i])
        for i, (source, target) in enumerate(zip((pos_hbm, k_hbm, v_hbm, q_hbm, g_hbm), targets))
    ]
    for copy in copies:
        copy.start()
    pos_ref, k_ref, v_ref, q_ref, g_ref = targets
    tok, width = q_ref.shape
    head = k_ref.shape[1]
    step = tok // len(out_refs)
    copies[0].wait()
    rank = rank_of(pos_ref, lax.axis_index("dcp"))[1]
    perm = (rank == lax.broadcasted_iota(jnp.int32, (tok, tok), 0)).astype(BF16)
    for side, ref in enumerate((k_ref, v_ref)):
        copies[1 + side].wait()
        ordered_ref[:, side * head : (side + 1) * head] = dot(perm, ref[...], ((1,), (0,))).astype(BF16)
    perm = (rank == group_rows(per_peer, paired, tok)).astype(BF16)
    for side, ref in enumerate((q_ref, g_ref)):
        copies[3 + side].wait()
        rows = dot(perm, ref[...], ((1,), (0,))).astype(BF16)
        for i, out_ref in enumerate(out_refs):
            out_ref[:, side * width : (side + 1) * width] = rows[i * step : (i + 1) * step]


def near_kernel(per_peer, paired, pairs, *refs):
    pair_refs, refs = refs[:pairs], refs[pairs:]
    near = len(refs) // 2
    step, base = refs[0].shape
    tok, two = pair_refs[0].shape
    want = group_rows(per_peer, paired, tok)[: near * step]
    lane = lax.broadcasted_iota(jnp.int32, want.shape, 1)
    for i in range(near):
        refs[near + i][:, :base] = refs[i][...]
    for block in range(SPAN + 1):
        perm = (lane == want + (block - SPAN) * per_peer).astype(BF16)
        for side, ref in enumerate(pair_refs):
            rows = dot(perm, ref[...], ((1,), (0,))).astype(BF16)
            first = base + two * (side * (SPAN + 1) + block)
            for i in range(near):
                refs[near + i][:, first : first + two] = rows[i * step : (i + 1) * step]


def far_kernel(place_ref, *refs):
    *in_refs, out_ref = refs
    rows = jnp.concatenate([ref[...] for ref in in_refs], axis=0)
    rows = jnp.concatenate([jnp.zeros_like(rows), rows], axis=0)
    out_ref[...] = dot(place_ref[SPAN * out_ref.shape[0] :, :], rows, ((1,), (0,))).astype(BF16)


def attend_kernel(width, head, pieces, mask_ref, place_ref, *refs):
    near = max(1, pieces // 2)
    in_refs = refs[:near]
    refs = refs[near:]
    if pieces > near:
        far_ref, *refs = refs
    key_ref, value_ref, prob_ref, ds_ref, own_ref, *part_refs = refs
    tok = key_ref.shape[0] // (SPAN + 1)
    heads = width // head
    me = lax.axis_index("dcp")
    scale = 1.0 / math.sqrt(head)
    factor = scale * math.log2(math.e)
    base = 2 * width
    def arrived(first, last):
        return jnp.concatenate([ref[:, first:last] for ref in in_refs], axis=0)

    def window(block):
        parts = []
        for side in range(pieces // near):
            first = base + 2 * head * (side * (SPAN + 1) + block)
            parts += [ref[:, first : first + 2 * head] for ref in in_refs[:near]]
        return jnp.concatenate(parts, axis=0)

    keys, values = [], []
    for block in range(SPAN + 1):
        place = place_ref[block * tok : (block + 1) * tok, :]
        both = dot(place, window(block), ((1,), (0,))).astype(BF16)
        keys.append(both[:, :head])
        values.append(both[:, head:])
    key = jnp.concatenate(keys, axis=0)
    value = jnp.concatenate(values, axis=0)
    key_ref[...] = key
    value_ref[...] = value
    def placed(first, last):
        rows = arrived(first, last)
        if pieces == near:
            return dot(place_ref[SPAN * tok :, :], rows, ((1,), (0,))).astype(BF16)
        rows = jnp.concatenate([rows, jnp.zeros_like(rows)], axis=0)
        rows = dot(place_ref[SPAN * tok :, :], rows, ((1,), (0,)))
        return (rows + far_ref[:, first:last].astype(F32)).astype(BF16)

    queries = placed(0, width)
    grads = placed(width, base)

    pairs = 4
    window_rows = (SPAN + 1) * tok
    mask = jnp.concatenate([mask_ref[...]] * pairs, axis=1)

    key_grad = jnp.zeros((window_rows, head), F32)
    value_grad = jnp.zeros((window_rows, head), F32)
    for first in range(0, heads, pairs):
        spans = [slice(h * head, (h + 1) * head) for h in range(first, first + pairs)]
        q_two = jnp.concatenate([queries[:, s] for s in spans], axis=0)
        g_two = jnp.concatenate([grads[:, s] for s in spans], axis=0)
        scores = dot(key, q_two, ((1,), (1,))) + mask
        top = jnp.max(scores, axis=0, keepdims=True)
        weights = jnp.exp2((scores - top) * factor)
        inverse = 1.0 / jnp.sum(weights, axis=0, keepdims=True)
        prob = weights * inverse
        prob_low = prob.astype(BF16)
        grad_prob = dot(value, g_two, ((1,), (1,)))
        delta = jnp.sum(prob * grad_prob, axis=0, keepdims=True)
        grad_score = (prob * (grad_prob - delta)).astype(BF16)
        value_grad += dot(prob_low, g_two, ((1,), (0,)))
        key_grad += dot(grad_score, q_two, ((1,), (0,)))
        prob_ref[:, first * tok : (first + pairs) * tok] = prob_low
        ds_ref[:, first * tok : (first + pairs) * tok] = grad_score
    key_grad = key_grad * scale
    own_ref[:, :head] = key_grad[SPAN * tok :, :]
    own_ref[:, head:] = value_grad[SPAN * tok :, :]
    for offset in range(1, SPAN + 1):
        rows = slice((SPAN - offset) * tok, (SPAN - offset + 1) * tok)
        part_refs[offset - 1][:, :head] = key_grad[rows, :].astype(BF16)
        part_refs[offset - 1][:, head:] = value_grad[rows, :].astype(BF16)


def output_kernel(key_ref, value_ref, prob_ref, ds_ref, attn_ref, dq_ref):
    tok, width = attn_ref.shape
    head = key_ref.shape[1]
    scale = 1.0 / math.sqrt(head)
    pairs = 4
    for first in range(0, width // head, pairs):
        cols = slice(first * tok, (first + pairs) * tok)
        out_t = dot(value_ref[...], prob_ref[:, cols], ((0,), (0,)))
        dq_t = dot(key_ref[...], ds_ref[:, cols], ((0,), (0,))) * scale
        for i in range(pairs):
            s = slice((first + i) * head, (first + i + 1) * head)
            attn_ref[:, s] = jnp.transpose(out_t[:, i * tok : (i + 1) * tok]).astype(BF16)
            dq_ref[:, s] = jnp.transpose(dq_t[:, i * tok : (i + 1) * tok]).astype(BF16)


def per_device(query, key, value, grad_out, loader_pos, doc_lengths):
    tok, width = query.shape
    head = key.shape[1]
    devices = lax.axis_size("dcp")
    per_peer = tok // devices
    vmem = pl.BlockSpec(memory_space=pltpu.VMEM)
    params = pltpu.CompilerParams(vmem_limit_bytes=48 << 20)
    hbm = pl.BlockSpec(memory_space=pltpu.HBM)
    base = 2 * width
    paired = devices <= 16 and devices & (devices - 1) == 0
    pieces = devices if paired else 1
    positions = pltpu.with_memory_space_constraint(loader_pos.reshape(devices, tok), pltpu.HBM)
    lengths = pltpu.with_memory_space_constraint(doc_lengths, pltpu.HBM)
    sides = [pltpu.with_memory_space_constraint(x, pltpu.HBM) for x in (query, key, value, grad_out)]
    near = max(1, pieces // 2)
    def swapped(rows, step):
        return lax.ppermute(rows, "dcp", [(d, d ^ step) for d in range(devices)])

    ordered, *packed = pl.pallas_call(
        functools.partial(pack_kernel, per_peer, paired),
        out_shape=[jax.ShapeDtypeStruct((tok, 2 * head), BF16)]
        + [jax.ShapeDtypeStruct((tok // pieces, base), BF16)] * pieces,
        in_specs=[hbm] * 5,
        out_specs=[vmem] * (1 + pieces),
        scratch_shapes=[
            pltpu.VMEM((devices, tok), jnp.int32),
            pltpu.VMEM(key.shape, BF16),
            pltpu.VMEM(value.shape, BF16),
            pltpu.VMEM(query.shape, BF16),
            pltpu.VMEM(grad_out.shape, BF16),
            pltpu.SemaphoreType.DMA((5,)),
        ],
        compiler_params=params,
        name="pack",
    )(positions, sides[1], sides[2], sides[0], sides[3])
    held = [ordered, swapped(ordered, near)] if paired else [ordered]
    for step in range(near, pieces if paired else 0):
        packed[step] = swapped(packed[step], step)
    cols = base + 2 * head * (SPAN + 1) * len(held)
    packed[:near] = pl.pallas_call(
        functools.partial(near_kernel, per_peer, paired, len(held)),
        out_shape=[jax.ShapeDtypeStruct((tok // pieces, cols), BF16)] * near,
        in_specs=[vmem] * (len(held) + near),
        out_specs=[vmem] * near,
        compiler_params=params,
        name="near",
    )(*held, *packed[:near])
    if paired:
        for step in range(1, near):
            packed[step] = swapped(packed[step], step)
    else:
        packed = [lax.all_to_all(packed[0], "dcp", split_axis=0, concat_axis=0, tiled=True)]
    places, mask = pl.pallas_call(
        functools.partial(slots_kernel, per_peer, paired),
        out_shape=[
            jax.ShapeDtypeStruct(((SPAN + 1) * tok, tok), BF16),
            jax.ShapeDtypeStruct(((SPAN + 1) * tok, tok), F32),
        ],
        in_specs=[hbm, hbm, pl.BlockSpec(memory_space=pl.ANY)],
        out_specs=[vmem] * 2,
        scratch_shapes=[
            pltpu.VMEM((devices, tok), jnp.int32),
            pltpu.SMEM(doc_lengths.shape, jnp.int32),
            pltpu.VMEM((tok, LANES), F32),
            pltpu.SemaphoreType.DMA((2,)),
        ],
        compiler_params=params,
        name="slots",
    )(positions, lengths, packed[0])
    wide = jax.ShapeDtypeStruct((tok, width), BF16)
    if paired:
        far = pl.pallas_call(
            far_kernel,
            out_shape=jax.ShapeDtypeStruct((tok, base), BF16),
            in_specs=[vmem] * (1 + pieces - near),
            out_specs=vmem,
            compiler_params=params,
            cost_estimate=pl.CostEstimate(flops=1 << 33, bytes_accessed=1 << 20, transcendentals=0),
            name="far",
        )(places, *packed[near:])
        packed[near:] = [far]
    rows = (SPAN + 1) * tok
    seen = jax.ShapeDtypeStruct((rows, head), BF16)
    square = jax.ShapeDtypeStruct((rows, tok * width // head), BF16)
    part = jax.ShapeDtypeStruct((tok, 2 * head), BF16)
    keys, values, probs, grad_scores, summed, *parts = pl.pallas_call(
        functools.partial(attend_kernel, width, head, pieces),
        out_shape=[seen, seen, square, square, jax.ShapeDtypeStruct((tok, 2 * head), F32)] + [part] * SPAN,
        in_specs=[vmem] * (2 + len(packed)),
        out_specs=[vmem] * (5 + SPAN),
        compiler_params=params,
        name="attend",
    )(mask, places, *packed)
    attn_out, dquery = pl.pallas_call(
        output_kernel,
        out_shape=[wide, wide],
        in_specs=[vmem] * 4,
        out_specs=[vmem] * 2,
        compiler_params=params,
        name="outputs",
    )(keys, values, probs, grad_scores)
    for offset in range(SPAN, 0, -1):
        pairs = [(source, source - offset) for source in range(offset, devices)]
        summed = summed + lax.ppermute(parts[offset - 1], "dcp", pairs).astype(F32)
    return attn_out, dquery, summed[:, :head].astype(BF16), summed[:, head:].astype(BF16)


def solution(mesh):
    rows = P(("rep", "dcp"), None)
    return jax.shard_map(
        per_device,
        mesh=mesh,
        in_specs=(rows, rows, rows, rows, P("rep"), P("rep")),
        out_specs=(rows, rows, rows, rows),
        check_vma=False,
    )
```

```python
import functools
import math

import jax
import jax.numpy as jnp
from jax import lax
from jax.experimental import pallas as pl
from jax.experimental.pallas import tpu as pltpu
from jax.sharding import PartitionSpec as P

SPAN = 5
LANES = 128
NEG = -1e30
F32 = jnp.float32
BF16 = jnp.bfloat16


def dot(a, b, dims):
    return lax.dot_general(a, b, (dims, ((), ())), preferred_element_type=F32)


def rank_of(pos_ref, device):
    tok = pos_ref.shape[1]
    pos_row = pos_ref[pl.ds(device, 1), :]
    pos_col = jnp.transpose(jnp.broadcast_to(pos_row, (tok, tok)))
    return pos_row, jnp.sum((pos_col < pos_row).astype(jnp.int32), axis=0, keepdims=True)


def slots_kernel(per_peer, paired, pos_hbm, len_hbm, _, place_ref, mask_ref, live_ref, pos_ref, len_ref, slot_ref, sems):
    copies = [
        pltpu.make_async_copy(pos_hbm, pos_ref, sems.at[0]),
        pltpu.make_async_copy(len_hbm, len_ref, sems.at[1]),
    ]
    for copy in copies:
        copy.start()
    devices, tok = pos_ref.shape
    me = lax.axis_index("dcp")
    rows = (SPAN + 1) * per_peer
    window = (me - SPAN) * per_peer + lax.broadcasted_iota(jnp.int32, (rows, tok), 0)
    lane = lax.broadcasted_iota(jnp.int32, (per_peer, LANES), 1)
    copies[0].wait()

    def slots_from(device):
        pos_row, rank = rank_of(pos_ref, device)
        slot = (pos_row % tok).astype(F32)
        column = jnp.sum(jnp.where(rank == window, slot, 0.0), axis=1, keepdims=True)
        slots = jnp.zeros((per_peer, LANES), F32)
        for block in range(SPAN + 1):
            slots = jnp.where(lane == block, column[block * per_peer : (block + 1) * per_peer], slots)
        return slots

    if devices <= 16:
        for source in range(devices):
            device = source ^ me if paired else source
            slot_ref[source * per_peer : (source + 1) * per_peer, :] = slots_from(device)
    else:

        @pl.loop(0, devices)
        def _(source):
            slot_ref[pl.ds(source * per_peer, per_peer), :] = slots_from(source)

    slot = lax.broadcasted_iota(jnp.int32, (tok, tok), 0).astype(F32)
    arrived = jnp.transpose(slot_ref[...])
    for block in range(SPAN + 1):
        rows = slice(block * tok, (block + 1) * tok)
        place_ref[rows, :] = (arrived[block : block + 1, :] == slot).astype(BF16)

    copies[1].wait()
    q_pos = me * tok + lax.broadcasted_iota(jnp.int32, (1, tok), 1)
    q_start = jnp.zeros((1, tok), jnp.int32)
    end = jnp.int32(0)
    earliest = jnp.int32(0)
    for doc in range(len_ref.shape[0]):
        end = end + len_ref[doc]
        q_start = jnp.where(q_pos >= end, end, q_start)
        earliest = jnp.where(me * tok >= end, end, earliest)
    live_ref[...] = jnp.full(live_ref.shape, me - earliest // tok + 1, jnp.int32).astype(F32)
    k_pos = (me - SPAN) * tok + lax.broadcasted_iota(jnp.int32, mask_ref.shape, 0)
    mask_ref[...] = jnp.where((k_pos >= q_start) & (k_pos <= q_pos), 0.0, NEG)


def group_rows(per_peer, paired, tok):
    want = lax.broadcasted_iota(jnp.int32, (tok, tok), 0)
    if paired:
        want = ((want // per_peer) ^ lax.axis_index("dcp")) * per_peer + want % per_peer
    return want


def pack_kernel(per_peer, paired, pos_hbm, k_hbm, v_hbm, q_hbm, g_hbm, *rest):
    ordered_ref, *out_refs = rest[:-6]
    *targets, sems = rest[-6:]
    copies = [
        pltpu.make_async_copy(source, target, sems.at[i])
        for i, (source, target) in enumerate(zip((pos_hbm, k_hbm, v_hbm, q_hbm, g_hbm), targets))
    ]
    for copy in copies:
        copy.start()
    pos_ref, k_ref, v_ref, q_ref, g_ref = targets
    tok, width = q_ref.shape
    head = k_ref.shape[1]
    step = tok // len(out_refs)
    copies[0].wait()
    rank = rank_of(pos_ref, lax.axis_index("dcp"))[1]
    perm = (rank == lax.broadcasted_iota(jnp.int32, (tok, tok), 0)).astype(BF16)
    for side, ref in enumerate((k_ref, v_ref)):
        copies[1 + side].wait()
        ordered_ref[:, side * head : (side + 1) * head] = dot(perm, ref[...], ((1,), (0,))).astype(BF16)
    perm = (rank == group_rows(per_peer, paired, tok)).astype(BF16)
    for side, ref in enumerate((q_ref, g_ref)):
        copies[3 + side].wait()
        rows = dot(perm, ref[...], ((1,), (0,))).astype(BF16)
        for i, out_ref in enumerate(out_refs):
            out_ref[:, side * width : (side + 1) * width] = rows[i * step : (i + 1) * step]


def near_kernel(per_peer, paired, pairs, *refs):
    pair_refs, refs = refs[:pairs], refs[pairs:]
    near = len(refs) // 2
    step, base = refs[0].shape
    tok, two = pair_refs[0].shape
    want = group_rows(per_peer, paired, tok)[: near * step]
    lane = lax.broadcasted_iota(jnp.int32, want.shape, 1)
    for i in range(near):
        refs[near + i][:, :base] = refs[i][...]
    for block in range(SPAN + 1):
        perm = (lane == want + (block - SPAN) * per_peer).astype(BF16)
        for side, ref in enumerate(pair_refs):
            rows = dot(perm, ref[...], ((1,), (0,))).astype(BF16)
            first = base + two * (side * (SPAN + 1) + block)
            for i in range(near):
                refs[near + i][:, first : first + two] = rows[i * step : (i + 1) * step]


def far_kernel(place_ref, *refs):
    *in_refs, out_ref = refs
    rows = jnp.concatenate([ref[...] for ref in in_refs], axis=0)
    rows = jnp.concatenate([jnp.zeros_like(rows), rows], axis=0)
    out_ref[...] = dot(place_ref[SPAN * out_ref.shape[0] :, :], rows, ((1,), (0,))).astype(BF16)


def attend_kernel(width, head, pieces, live_ref, mask_ref, place_ref, *refs):
    near = max(1, pieces // 2)
    in_refs = refs[:near]
    refs = refs[near:]
    if pieces > near:
        far_ref, *refs = refs
    key_ref, value_ref, prob_ref, ds_ref, own_ref, *part_refs = refs
    tok = key_ref.shape[0] // (SPAN + 1)
    heads = width // head
    me = lax.axis_index("dcp")
    scale = 1.0 / math.sqrt(head)
    factor = scale * math.log2(math.e)
    base = 2 * width
    def arrived(first, last):
        return jnp.concatenate([ref[:, first:last] for ref in in_refs], axis=0)

    def window(block):
        parts = []
        for side in range(pieces // near):
            first = base + 2 * head * (side * (SPAN + 1) + block)
            parts += [ref[:, first : first + 2 * head] for ref in in_refs[:near]]
        return jnp.concatenate(parts, axis=0)

    def placed(first, last):
        rows = arrived(first, last)
        if pieces == near:
            return dot(place_ref[SPAN * tok :, :], rows, ((1,), (0,))).astype(BF16)
        rows = jnp.concatenate([rows, jnp.zeros_like(rows)], axis=0)
        rows = dot(place_ref[SPAN * tok :, :], rows, ((1,), (0,)))
        return (rows + far_ref[:, first:last].astype(F32)).astype(BF16)

    queries = placed(0, width)
    grads = placed(width, base)

    live = jnp.max(live_ref[...])

    def attend(skipped):
        dead = skipped * tok
        for ref in (key_ref, value_ref, prob_ref, ds_ref):
            if dead:
                ref[:dead, :] = jnp.zeros((dead, ref.shape[1]), BF16)
        for block in range(skipped, SPAN + 1):
            rows = slice(block * tok, (block + 1) * tok)
            both = dot(place_ref[rows, :], window(block), ((1,), (0,))).astype(BF16)
            key_ref[rows, :] = both[:, :head]
            value_ref[rows, :] = both[:, head:]
        key = key_ref[dead:, :]
        value = value_ref[dead:, :]
        pairs = 4
        mask = jnp.concatenate([mask_ref[dead:, :]] * pairs, axis=1)
        key_grad = jnp.zeros(key.shape, F32)
        value_grad = jnp.zeros(key.shape, F32)
        for first in range(0, heads, pairs):
            spans = [slice(h * head, (h + 1) * head) for h in range(first, first + pairs)]
            q_two = jnp.concatenate([queries[:, s] for s in spans], axis=0)
            g_two = jnp.concatenate([grads[:, s] for s in spans], axis=0)
            scores = dot(key, q_two, ((1,), (1,))) + mask
            top = jnp.max(scores, axis=0, keepdims=True)
            weights = jnp.exp2((scores - top) * factor)
            inverse = 1.0 / jnp.sum(weights, axis=0, keepdims=True)
            prob = weights * inverse
            prob_low = prob.astype(BF16)
            grad_prob = dot(value, g_two, ((1,), (1,)))
            delta = jnp.sum(prob * grad_prob, axis=0, keepdims=True)
            grad_score = (prob * (grad_prob - delta)).astype(BF16)
            value_grad += dot(prob_low, g_two, ((1,), (0,)))
            key_grad += dot(grad_score, q_two, ((1,), (0,)))
            prob_ref[dead:, first * tok : (first + pairs) * tok] = prob_low
            ds_ref[dead:, first * tok : (first + pairs) * tok] = grad_score
        key_grad = key_grad * scale
        for offset, ref in enumerate((own_ref, *part_refs)):
            block = SPAN - offset - skipped
            if block < 0:
                ref[...] = jnp.zeros(ref.shape, ref.dtype)
            else:
                rows = slice(block * tok, (block + 1) * tok)
                ref[:, :head] = key_grad[rows, :].astype(ref.dtype)
                ref[:, head:] = value_grad[rows, :].astype(ref.dtype)

    pl.when(live <= 2)(lambda: attend(SPAN - 1))
    pl.when((live > 2) & (live <= 4))(lambda: attend(SPAN - 3))
    pl.when(live > 4)(lambda: attend(0))


def output_kernel(key_ref, value_ref, prob_ref, ds_ref, attn_ref, dq_ref):
    tok, width = attn_ref.shape
    head = key_ref.shape[1]
    scale = 1.0 / math.sqrt(head)
    pairs = 4
    for first in range(0, width // head, pairs):
        cols = slice(first * tok, (first + pairs) * tok)
        out_t = dot(value_ref[...], prob_ref[:, cols], ((0,), (0,)))
        dq_t = dot(key_ref[...], ds_ref[:, cols], ((0,), (0,))) * scale
        for i in range(pairs):
            s = slice((first + i) * head, (first + i + 1) * head)
            attn_ref[:, s] = jnp.transpose(out_t[:, i * tok : (i + 1) * tok]).astype(BF16)
            dq_ref[:, s] = jnp.transpose(dq_t[:, i * tok : (i + 1) * tok]).astype(BF16)


def per_device(query, key, value, grad_out, loader_pos, doc_lengths):
    tok, width = query.shape
    head = key.shape[1]
    devices = lax.axis_size("dcp")
    per_peer = tok // devices
    vmem = pl.BlockSpec(memory_space=pltpu.VMEM)
    params = pltpu.CompilerParams(vmem_limit_bytes=48 << 20)
    hbm = pl.BlockSpec(memory_space=pltpu.HBM)
    base = 2 * width
    paired = devices <= 16 and devices & (devices - 1) == 0
    pieces = devices if paired else 1
    positions = pltpu.with_memory_space_constraint(loader_pos.reshape(devices, tok), pltpu.HBM)
    lengths = pltpu.with_memory_space_constraint(doc_lengths, pltpu.HBM)
    sides = [pltpu.with_memory_space_constraint(x, pltpu.HBM) for x in (query, key, value, grad_out)]
    near = max(1, pieces // 2)
    def swapped(rows, step):
        return lax.ppermute(rows, "dcp", [(d, d ^ step) for d in range(devices)])

    ordered, *packed = pl.pallas_call(
        functools.partial(pack_kernel, per_peer, paired),
        out_shape=[jax.ShapeDtypeStruct((tok, 2 * head), BF16)]
        + [jax.ShapeDtypeStruct((tok // pieces, base), BF16)] * pieces,
        in_specs=[hbm] * 5,
        out_specs=[vmem] * (1 + pieces),
        scratch_shapes=[
            pltpu.VMEM((devices, tok), jnp.int32),
            pltpu.VMEM(key.shape, BF16),
            pltpu.VMEM(value.shape, BF16),
            pltpu.VMEM(query.shape, BF16),
            pltpu.VMEM(grad_out.shape, BF16),
            pltpu.SemaphoreType.DMA((5,)),
        ],
        compiler_params=params,
        name="pack",
    )(positions, sides[1], sides[2], sides[0], sides[3])
    held = [ordered, swapped(ordered, near)] if paired else [ordered]
    for step in range(near, pieces if paired else 0):
        packed[step] = swapped(packed[step], step)
    cols = base + 2 * head * (SPAN + 1) * len(held)
    packed[:near] = pl.pallas_call(
        functools.partial(near_kernel, per_peer, paired, len(held)),
        out_shape=[jax.ShapeDtypeStruct((tok // pieces, cols), BF16)] * near,
        in_specs=[vmem] * (len(held) + near),
        out_specs=[vmem] * near,
        compiler_params=params,
        name="near",
    )(*held, *packed[:near])
    if paired:
        for step in range(1, near):
            packed[step] = swapped(packed[step], step)
    else:
        packed = [lax.all_to_all(packed[0], "dcp", split_axis=0, concat_axis=0, tiled=True)]
    places, mask, live = pl.pallas_call(
        functools.partial(slots_kernel, per_peer, paired),
        out_shape=[
            jax.ShapeDtypeStruct(((SPAN + 1) * tok, tok), BF16),
            jax.ShapeDtypeStruct(((SPAN + 1) * tok, tok), F32),
            jax.ShapeDtypeStruct((8, LANES), F32),
        ],
        in_specs=[hbm, hbm, pl.BlockSpec(memory_space=pl.ANY)],
        out_specs=[vmem] * 3,
        scratch_shapes=[
            pltpu.VMEM((devices, tok), jnp.int32),
            pltpu.SMEM(doc_lengths.shape, jnp.int32),
            pltpu.VMEM((tok, LANES), F32),
            pltpu.SemaphoreType.DMA((2,)),
        ],
        compiler_params=params,
        name="slots",
    )(positions, lengths, packed[0])
    wide = jax.ShapeDtypeStruct((tok, width), BF16)
    if paired:
        far = pl.pallas_call(
            far_kernel,
            out_shape=jax.ShapeDtypeStruct((tok, base), BF16),
            in_specs=[vmem] * (1 + pieces - near),
            out_specs=vmem,
            compiler_params=params,
            cost_estimate=pl.CostEstimate(flops=1 << 33, bytes_accessed=1 << 20, transcendentals=0),
            name="far",
        )(places, *packed[near:])
        packed[near:] = [far]
    rows = (SPAN + 1) * tok
    seen = jax.ShapeDtypeStruct((rows, head), BF16)
    square = jax.ShapeDtypeStruct((rows, tok * width // head), BF16)
    part = jax.ShapeDtypeStruct((tok, 2 * head), BF16)
    keys, values, probs, grad_scores, summed, *parts = pl.pallas_call(
        functools.partial(attend_kernel, width, head, pieces),
        out_shape=[seen, seen, square, square, jax.ShapeDtypeStruct((tok, 2 * head), F32)] + [part] * SPAN,
        in_specs=[vmem] * (3 + len(packed)),
        out_specs=[vmem] * (5 + SPAN),
        compiler_params=params,
        name="attend",
    )(live, mask, places, *packed)
    attn_out, dquery = pl.pallas_call(
        output_kernel,
        out_shape=[wide, wide],
        in_specs=[vmem] * 4,
        out_specs=[vmem] * 2,
        compiler_params=params,
        name="outputs",
    )(keys, values, probs, grad_scores)
    for offset in range(SPAN, 0, -1):
        pairs = [(source, source - offset) for source in range(offset, devices)]
        summed = summed + lax.ppermute(parts[offset - 1], "dcp", pairs).astype(F32)
    return attn_out, dquery, summed[:, :head].astype(BF16), summed[:, head:].astype(BF16)


def solution(mesh):
    rows = P(("rep", "dcp"), None)
    return jax.shard_map(
        per_device,
        mesh=mesh,
        in_specs=(rows, rows, rows, rows, P("rep"), P("rep")),
        out_specs=(rows, rows, rows, rows),
        check_vma=False,
    )
```

```python
import functools
import math

import jax
import jax.numpy as jnp
from jax import lax
from jax.experimental import pallas as pl
from jax.experimental.pallas import tpu as pltpu
from jax.sharding import PartitionSpec as P

SPAN = 5
LANES = 128
NEG = -1e30
F32 = jnp.float32
BF16 = jnp.bfloat16


def dot(a, b, dims):
    return lax.dot_general(a, b, (dims, ((), ())), preferred_element_type=F32)


def rank_of(pos_ref, device):
    tok = pos_ref.shape[1]
    pos_row = pos_ref[pl.ds(device, 1), :]
    pos_col = jnp.transpose(jnp.broadcast_to(pos_row, (tok, tok)))
    return pos_row, jnp.sum((pos_col < pos_row).astype(jnp.int32), axis=0, keepdims=True)


def slots_kernel(per_peer, paired, pos_hbm, len_hbm, _, place_ref, mask_ref, live_ref, pos_ref, len_ref, slot_ref, sems):
    copies = [
        pltpu.make_async_copy(pos_hbm, pos_ref, sems.at[0]),
        pltpu.make_async_copy(len_hbm, len_ref, sems.at[1]),
    ]
    for copy in copies:
        copy.start()
    devices, tok = pos_ref.shape
    me = lax.axis_index("dcp")
    rows = (SPAN + 1) * per_peer
    window = (me - SPAN) * per_peer + lax.broadcasted_iota(jnp.int32, (rows, tok), 0)
    lane = lax.broadcasted_iota(jnp.int32, (per_peer, LANES), 1)
    copies[0].wait()

    def slots_from(device):
        pos_row, rank = rank_of(pos_ref, device)
        slot = (pos_row % tok).astype(F32)
        column = jnp.sum(jnp.where(rank == window, slot, 0.0), axis=1, keepdims=True)
        slots = jnp.zeros((per_peer, LANES), F32)
        for block in range(SPAN + 1):
            slots = jnp.where(lane == block, column[block * per_peer : (block + 1) * per_peer], slots)
        return slots

    if devices <= 16:
        for source in range(devices):
            device = source ^ me if paired else source
            slot_ref[source * per_peer : (source + 1) * per_peer, :] = slots_from(device)
    else:

        @pl.loop(0, devices)
        def _(source):
            slot_ref[pl.ds(source * per_peer, per_peer), :] = slots_from(source)

    slot = lax.broadcasted_iota(jnp.int32, (tok, tok), 0).astype(F32)
    arrived = jnp.transpose(slot_ref[...])
    for block in range(SPAN + 1):
        rows = slice(block * tok, (block + 1) * tok)
        place_ref[rows, :] = (arrived[block : block + 1, :] == slot).astype(BF16)

    copies[1].wait()
    q_pos = me * tok + lax.broadcasted_iota(jnp.int32, (1, tok), 1)
    q_start = jnp.zeros((1, tok), jnp.int32)
    end = jnp.int32(0)
    earliest = jnp.int32(0)
    for doc in range(len_ref.shape[0]):
        end = end + len_ref[doc]
        q_start = jnp.where(q_pos >= end, end, q_start)
        earliest = jnp.where(me * tok >= end, end, earliest)
    live_ref[...] = jnp.full(live_ref.shape, me - earliest // tok + 1, jnp.int32).astype(F32)
    k_pos = (me - SPAN) * tok + lax.broadcasted_iota(jnp.int32, mask_ref.shape, 0)
    mask_ref[...] = jnp.where((k_pos >= q_start) & (k_pos <= q_pos), 0.0, NEG)


def group_rows(per_peer, paired, tok):
    want = lax.broadcasted_iota(jnp.int32, (tok, tok), 0)
    if paired:
        want = ((want // per_peer) ^ lax.axis_index("dcp")) * per_peer + want % per_peer
    return want


def pack_kernel(per_peer, paired, pos_hbm, k_hbm, v_hbm, q_hbm, g_hbm, *rest):
    ordered_ref, *out_refs = rest[:-6]
    *targets, sems = rest[-6:]
    copies = [
        pltpu.make_async_copy(source, target, sems.at[i])
        for i, (source, target) in enumerate(zip((pos_hbm, k_hbm, v_hbm, q_hbm, g_hbm), targets))
    ]
    for copy in copies:
        copy.start()
    pos_ref, k_ref, v_ref, q_ref, g_ref = targets
    tok, width = q_ref.shape
    head = k_ref.shape[1]
    step = tok // len(out_refs)
    copies[0].wait()
    rank = rank_of(pos_ref, lax.axis_index("dcp"))[1]
    perm = (rank == lax.broadcasted_iota(jnp.int32, (tok, tok), 0)).astype(BF16)
    for side, ref in enumerate((k_ref, v_ref)):
        copies[1 + side].wait()
        ordered_ref[:, side * head : (side + 1) * head] = dot(perm, ref[...], ((1,), (0,))).astype(BF16)
    perm = (rank == group_rows(per_peer, paired, tok)).astype(BF16)
    for side, ref in enumerate((q_ref, g_ref)):
        copies[3 + side].wait()
        rows = dot(perm, ref[...], ((1,), (0,))).astype(BF16)
        for i, out_ref in enumerate(out_refs):
            out_ref[:, side * width : (side + 1) * width] = rows[i * step : (i + 1) * step]


def near_kernel(per_peer, paired, pairs, *refs):
    pair_refs, refs = refs[:pairs], refs[pairs:]
    near = len(refs) // 2
    step, base = refs[0].shape
    tok, two = pair_refs[0].shape
    want = group_rows(per_peer, paired, tok)[: near * step]
    lane = lax.broadcasted_iota(jnp.int32, want.shape, 1)
    for i in range(near):
        refs[near + i][:, :base] = refs[i][...]
    for block in range(SPAN + 1):
        perm = (lane == want + (block - SPAN) * per_peer).astype(BF16)
        for side, ref in enumerate(pair_refs):
            rows = dot(perm, ref[...], ((1,), (0,))).astype(BF16)
            first = base + two * (side * (SPAN + 1) + block)
            for i in range(near):
                refs[near + i][:, first : first + two] = rows[i * step : (i + 1) * step]


def far_kernel(place_ref, *refs):
    *in_refs, out_ref = refs
    rows = jnp.concatenate([ref[...] for ref in in_refs], axis=0)
    rows = jnp.concatenate([jnp.zeros_like(rows), rows], axis=0)
    out_ref[...] = dot(place_ref[SPAN * out_ref.shape[0] :, :], rows, ((1,), (0,))).astype(BF16)


def attend_kernel(width, head, pieces, live_ref, mask_ref, place_ref, *refs):
    near = max(1, pieces // 2)
    in_refs = refs[:near]
    refs = refs[near:]
    if pieces > near:
        far_ref, *refs = refs
    key_ref, value_ref, prob_ref, ds_ref, own_ref, *part_refs = refs
    tok = key_ref.shape[0] // (SPAN + 1)
    heads = width // head
    me = lax.axis_index("dcp")
    scale = 1.0 / math.sqrt(head)
    factor = scale * math.log2(math.e)
    base = 2 * width
    def arrived(first, last):
        return jnp.concatenate([ref[:, first:last] for ref in in_refs], axis=0)

    def window(block):
        parts = []
        for side in range(pieces // near):
            first = base + 2 * head * (side * (SPAN + 1) + block)
            parts += [ref[:, first : first + 2 * head] for ref in in_refs[:near]]
        return jnp.concatenate(parts, axis=0)

    def placed(first, last):
        rows = arrived(first, last)
        if pieces == near:
            return dot(place_ref[SPAN * tok :, :], rows, ((1,), (0,))).astype(BF16)
        rows = jnp.concatenate([rows, jnp.zeros_like(rows)], axis=0)
        rows = dot(place_ref[SPAN * tok :, :], rows, ((1,), (0,)))
        return (rows + far_ref[:, first:last].astype(F32)).astype(BF16)

    queries = placed(0, width)
    grads = placed(width, base)

    live = jnp.max(live_ref[...])

    def attend(skipped):
        dead = skipped * tok
        for ref in (key_ref, value_ref, prob_ref, ds_ref):
            if dead:
                ref[:dead, :] = jnp.zeros((dead, ref.shape[1]), BF16)
        for block in range(skipped, SPAN + 1):
            rows = slice(block * tok, (block + 1) * tok)
            both = dot(place_ref[rows, :], window(block), ((1,), (0,))).astype(BF16)
            key_ref[rows, :] = both[:, :head]
            value_ref[rows, :] = both[:, head:]
        key = key_ref[dead:, :]
        value = value_ref[dead:, :]
        pairs = 4
        mask = jnp.concatenate([mask_ref[dead:, :]] * pairs, axis=1)
        key_grad = jnp.zeros(key.shape, F32)
        value_grad = jnp.zeros(key.shape, F32)
        for first in range(0, heads, pairs):
            spans = [slice(h * head, (h + 1) * head) for h in range(first, first + pairs)]
            q_two = jnp.concatenate([queries[:, s] for s in spans], axis=0)
            g_two = jnp.concatenate([grads[:, s] for s in spans], axis=0)
            scores = dot(key, q_two, ((1,), (1,))) + mask
            top = jnp.max(scores, axis=0, keepdims=True)
            weights = jnp.exp2((scores - top) * factor)
            inverse = 1.0 / jnp.sum(weights, axis=0, keepdims=True)
            prob = weights * inverse
            prob_low = prob.astype(BF16)
            grad_prob = dot(value, g_two, ((1,), (1,)))
            delta = jnp.sum(prob * grad_prob, axis=0, keepdims=True)
            grad_score = (prob * (grad_prob - delta)).astype(BF16)
            value_grad += dot(prob_low, g_two, ((1,), (0,)))
            key_grad += dot(grad_score, q_two, ((1,), (0,)))
            prob_ref[dead:, first * tok : (first + pairs) * tok] = prob_low
            ds_ref[dead:, first * tok : (first + pairs) * tok] = grad_score
        key_grad = key_grad * scale
        for offset, ref in enumerate((own_ref, *part_refs)):
            block = SPAN - offset - skipped
            if block < 0:
                ref[...] = jnp.zeros(ref.shape, ref.dtype)
            else:
                rows = slice(block * tok, (block + 1) * tok)
                ref[:, :head] = key_grad[rows, :].astype(ref.dtype)
                ref[:, head:] = value_grad[rows, :].astype(ref.dtype)

    pl.when(live > SPAN)(lambda: attend(0))
    for skipped in range(1, SPAN + 1):
        pl.when(live == SPAN + 1 - skipped)(functools.partial(attend, skipped))


def output_kernel(key_ref, value_ref, prob_ref, ds_ref, attn_ref, dq_ref):
    tok, width = attn_ref.shape
    head = key_ref.shape[1]
    scale = 1.0 / math.sqrt(head)
    pairs = 4
    for first in range(0, width // head, pairs):
        cols = slice(first * tok, (first + pairs) * tok)
        out_t = dot(value_ref[...], prob_ref[:, cols], ((0,), (0,)))
        dq_t = dot(key_ref[...], ds_ref[:, cols], ((0,), (0,))) * scale
        for i in range(pairs):
            s = slice((first + i) * head, (first + i + 1) * head)
            attn_ref[:, s] = jnp.transpose(out_t[:, i * tok : (i + 1) * tok]).astype(BF16)
            dq_ref[:, s] = jnp.transpose(dq_t[:, i * tok : (i + 1) * tok]).astype(BF16)


def per_device(query, key, value, grad_out, loader_pos, doc_lengths):
    tok, width = query.shape
    head = key.shape[1]
    devices = lax.axis_size("dcp")
    per_peer = tok // devices
    vmem = pl.BlockSpec(memory_space=pltpu.VMEM)
    params = pltpu.CompilerParams(vmem_limit_bytes=48 << 20)
    hbm = pl.BlockSpec(memory_space=pltpu.HBM)
    base = 2 * width
    paired = devices <= 16 and devices & (devices - 1) == 0
    pieces = devices if paired else 1
    positions = pltpu.with_memory_space_constraint(loader_pos.reshape(devices, tok), pltpu.HBM)
    lengths = pltpu.with_memory_space_constraint(doc_lengths, pltpu.HBM)
    sides = [pltpu.with_memory_space_constraint(x, pltpu.HBM) for x in (query, key, value, grad_out)]
    near = max(1, pieces // 2)
    def swapped(rows, step):
        return lax.ppermute(rows, "dcp", [(d, d ^ step) for d in range(devices)])

    ordered, *packed = pl.pallas_call(
        functools.partial(pack_kernel, per_peer, paired),
        out_shape=[jax.ShapeDtypeStruct((tok, 2 * head), BF16)]
        + [jax.ShapeDtypeStruct((tok // pieces, base), BF16)] * pieces,
        in_specs=[hbm] * 5,
        out_specs=[vmem] * (1 + pieces),
        scratch_shapes=[
            pltpu.VMEM((devices, tok), jnp.int32),
            pltpu.VMEM(key.shape, BF16),
            pltpu.VMEM(value.shape, BF16),
            pltpu.VMEM(query.shape, BF16),
            pltpu.VMEM(grad_out.shape, BF16),
            pltpu.SemaphoreType.DMA((5,)),
        ],
        compiler_params=params,
        name="pack",
    )(positions, sides[1], sides[2], sides[0], sides[3])
    held = [ordered, swapped(ordered, near)] if paired else [ordered]
    for step in range(near, pieces if paired else 0):
        packed[step] = swapped(packed[step], step)
    cols = base + 2 * head * (SPAN + 1) * len(held)
    packed[:near] = pl.pallas_call(
        functools.partial(near_kernel, per_peer, paired, len(held)),
        out_shape=[jax.ShapeDtypeStruct((tok // pieces, cols), BF16)] * near,
        in_specs=[vmem] * (len(held) + near),
        out_specs=[vmem] * near,
        compiler_params=params,
        name="near",
    )(*held, *packed[:near])
    if paired:
        for step in range(1, near):
            packed[step] = swapped(packed[step], step)
    else:
        packed = [lax.all_to_all(packed[0], "dcp", split_axis=0, concat_axis=0, tiled=True)]
    places, mask, live = pl.pallas_call(
        functools.partial(slots_kernel, per_peer, paired),
        out_shape=[
            jax.ShapeDtypeStruct(((SPAN + 1) * tok, tok), BF16),
            jax.ShapeDtypeStruct(((SPAN + 1) * tok, tok), F32),
            jax.ShapeDtypeStruct((8, LANES), F32),
        ],
        in_specs=[hbm, hbm, pl.BlockSpec(memory_space=pl.ANY)],
        out_specs=[vmem] * 3,
        scratch_shapes=[
            pltpu.VMEM((devices, tok), jnp.int32),
            pltpu.SMEM(doc_lengths.shape, jnp.int32),
            pltpu.VMEM((tok, LANES), F32),
            pltpu.SemaphoreType.DMA((2,)),
        ],
        compiler_params=params,
        name="slots",
    )(positions, lengths, packed[0])
    wide = jax.ShapeDtypeStruct((tok, width), BF16)
    if paired:
        far = pl.pallas_call(
            far_kernel,
            out_shape=jax.ShapeDtypeStruct((tok, base), BF16),
            in_specs=[vmem] * (1 + pieces - near),
            out_specs=vmem,
            compiler_params=params,
            cost_estimate=pl.CostEstimate(flops=1 << 33, bytes_accessed=1 << 20, transcendentals=0),
            name="far",
        )(places, *packed[near:])
        packed[near:] = [far]
    rows = (SPAN + 1) * tok
    seen = jax.ShapeDtypeStruct((rows, head), BF16)
    square = jax.ShapeDtypeStruct((rows, tok * width // head), BF16)
    part = jax.ShapeDtypeStruct((tok, 2 * head), BF16)
    keys, values, probs, grad_scores, summed, *parts = pl.pallas_call(
        functools.partial(attend_kernel, width, head, pieces),
        out_shape=[seen, seen, square, square, jax.ShapeDtypeStruct((tok, 2 * head), F32)] + [part] * SPAN,
        in_specs=[vmem] * (3 + len(packed)),
        out_specs=[vmem] * (5 + SPAN),
        compiler_params=params,
        name="attend",
    )(live, mask, places, *packed)
    attn_out, dquery = pl.pallas_call(
        output_kernel,
        out_shape=[wide, wide],
        in_specs=[vmem] * 4,
        out_specs=[vmem] * 2,
        compiler_params=params,
        name="outputs",
    )(keys, values, probs, grad_scores)
    for offset in range(SPAN, 0, -1):
        pairs = [(source, source - offset) for source in range(offset, devices)]
        summed = summed + lax.ppermute(parts[offset - 1], "dcp", pairs).astype(F32)
    return attn_out, dquery, summed[:, :head].astype(BF16), summed[:, head:].astype(BF16)


def solution(mesh):
    rows = P(("rep", "dcp"), None)
    return jax.shard_map(
        per_device,
        mesh=mesh,
        in_specs=(rows, rows, rows, rows, P("rep"), P("rep")),
        out_specs=(rows, rows, rows, rows),
        check_vma=False,
    )
```

```python
import functools
import math

import jax
import jax.numpy as jnp
from jax import lax
from jax.experimental import pallas as pl
from jax.experimental.pallas import tpu as pltpu
from jax.sharding import PartitionSpec as P

SPAN = 5
LANES = 128
NEG = -1e30
F32 = jnp.float32
BF16 = jnp.bfloat16


def dot(a, b, dims):
    return lax.dot_general(a, b, (dims, ((), ())), preferred_element_type=F32)


def rank_of(pos_ref, device):
    tok = pos_ref.shape[1]
    pos_row = pos_ref[pl.ds(device, 1), :]
    pos_col = jnp.transpose(jnp.broadcast_to(pos_row, (tok, tok)))
    return pos_row, jnp.sum((pos_col < pos_row).astype(jnp.int32), axis=0, keepdims=True)


def slots_kernel(per_peer, paired, pos_hbm, len_hbm, _, place_ref, mask_ref, live_ref, pos_ref, len_ref, slot_ref, sems):
    copies = [
        pltpu.make_async_copy(pos_hbm, pos_ref, sems.at[0]),
        pltpu.make_async_copy(len_hbm, len_ref, sems.at[1]),
    ]
    for copy in copies:
        copy.start()
    devices, tok = pos_ref.shape
    me = lax.axis_index("dcp")
    rows = (SPAN + 1) * per_peer
    window = (me - SPAN) * per_peer + lax.broadcasted_iota(jnp.int32, (rows, tok), 0)
    lane = lax.broadcasted_iota(jnp.int32, (per_peer, LANES), 1)
    copies[0].wait()

    def slots_from(device):
        pos_row, rank = rank_of(pos_ref, device)
        slot = (pos_row % tok).astype(F32)
        column = jnp.sum(jnp.where(rank == window, slot, 0.0), axis=1, keepdims=True)
        slots = jnp.zeros((per_peer, LANES), F32)
        for block in range(SPAN + 1):
            slots = jnp.where(lane == block, column[block * per_peer : (block + 1) * per_peer], slots)
        return slots

    if devices <= 16:
        for source in range(devices):
            device = source ^ me if paired else source
            slot_ref[source * per_peer : (source + 1) * per_peer, :] = slots_from(device)
    else:

        @pl.loop(0, devices)
        def _(source):
            slot_ref[pl.ds(source * per_peer, per_peer), :] = slots_from(source)

    slot = lax.broadcasted_iota(jnp.int32, (tok, tok), 0).astype(F32)
    arrived = jnp.transpose(slot_ref[...])
    for block in range(SPAN + 1):
        rows = slice(block * tok, (block + 1) * tok)
        place_ref[rows, :] = (arrived[block : block + 1, :] == slot).astype(BF16)

    copies[1].wait()
    q_pos = me * tok + lax.broadcasted_iota(jnp.int32, (1, tok), 1)
    q_start = jnp.zeros((1, tok), jnp.int32)
    end = jnp.int32(0)
    earliest = jnp.int32(0)
    for doc in range(len_ref.shape[0]):
        end = end + len_ref[doc]
        q_start = jnp.where(q_pos >= end, end, q_start)
        earliest = jnp.where(me * tok >= end, end, earliest)
    live_ref[...] = jnp.full(live_ref.shape, me - earliest // tok + 1, jnp.int32).astype(F32)
    k_pos = (me - SPAN) * tok + lax.broadcasted_iota(jnp.int32, mask_ref.shape, 0)
    mask_ref[...] = jnp.where((k_pos >= q_start) & (k_pos <= q_pos), 0.0, NEG)


def group_rows(per_peer, paired, tok):
    want = lax.broadcasted_iota(jnp.int32, (tok, tok), 0)
    if paired:
        want = ((want // per_peer) ^ lax.axis_index("dcp")) * per_peer + want % per_peer
    return want


def pack_kernel(per_peer, paired, pos_hbm, k_hbm, v_hbm, q_hbm, g_hbm, *rest):
    ordered_ref, *out_refs = rest[:-6]
    *targets, sems = rest[-6:]
    copies = [
        pltpu.make_async_copy(source, target, sems.at[i])
        for i, (source, target) in enumerate(zip((pos_hbm, k_hbm, v_hbm, q_hbm, g_hbm), targets))
    ]
    for copy in copies:
        copy.start()
    pos_ref, k_ref, v_ref, q_ref, g_ref = targets
    tok, width = q_ref.shape
    head = k_ref.shape[1]
    step = tok // len(out_refs)
    copies[0].wait()
    rank = rank_of(pos_ref, lax.axis_index("dcp"))[1]
    perm = (rank == lax.broadcasted_iota(jnp.int32, (tok, tok), 0)).astype(BF16)
    for side, ref in enumerate((k_ref, v_ref)):
        copies[1 + side].wait()
        ordered_ref[:, side * head : (side + 1) * head] = dot(perm, ref[...], ((1,), (0,))).astype(BF16)
    perm = (rank == group_rows(per_peer, paired, tok)).astype(BF16)
    for side, ref in enumerate((q_ref, g_ref)):
        copies[3 + side].wait()
        rows = dot(perm, ref[...], ((1,), (0,))).astype(BF16)
        for i, out_ref in enumerate(out_refs):
            out_ref[:, side * width : (side + 1) * width] = rows[i * step : (i + 1) * step]


def near_kernel(per_peer, paired, pairs, *refs):
    pair_refs, refs = refs[:pairs], refs[pairs:]
    near = len(refs) // 2
    step, base = refs[0].shape
    tok, two = pair_refs[0].shape
    want = group_rows(per_peer, paired, tok)[: near * step]
    lane = lax.broadcasted_iota(jnp.int32, want.shape, 1)
    for i in range(near):
        refs[near + i][:, :base] = refs[i][...]
    for block in range(SPAN + 1):
        perm = (lane == want + (block - SPAN) * per_peer).astype(BF16)
        for side, ref in enumerate(pair_refs):
            rows = dot(perm, ref[...], ((1,), (0,))).astype(BF16)
            first = base + two * (side * (SPAN + 1) + block)
            for i in range(near):
                refs[near + i][:, first : first + two] = rows[i * step : (i + 1) * step]


def far_kernel(place_ref, *refs):
    *in_refs, out_ref = refs
    rows = jnp.concatenate([ref[...] for ref in in_refs], axis=0)
    rows = jnp.concatenate([jnp.zeros_like(rows), rows], axis=0)
    out_ref[...] = dot(place_ref[SPAN * out_ref.shape[0] :, :], rows, ((1,), (0,))).astype(BF16)


def for_live(live_ref, body):
    live = jnp.max(live_ref[...])
    pl.when(live > SPAN)(lambda: body(0))
    for skipped in range(1, SPAN + 1):
        pl.when(live == SPAN + 1 - skipped)(functools.partial(body, skipped))


def attend_kernel(width, head, pieces, live_ref, mask_ref, place_ref, *refs):
    near = max(1, pieces // 2)
    in_refs = refs[:near]
    refs = refs[near:]
    if pieces > near:
        far_ref, *refs = refs
    key_ref, value_ref, prob_ref, ds_ref, own_ref, *part_refs = refs
    tok = key_ref.shape[0] // (SPAN + 1)
    heads = width // head
    me = lax.axis_index("dcp")
    scale = 1.0 / math.sqrt(head)
    factor = scale * math.log2(math.e)
    base = 2 * width
    def arrived(first, last):
        return jnp.concatenate([ref[:, first:last] for ref in in_refs], axis=0)

    def window(block):
        parts = []
        for side in range(pieces // near):
            first = base + 2 * head * (side * (SPAN + 1) + block)
            parts += [ref[:, first : first + 2 * head] for ref in in_refs[:near]]
        return jnp.concatenate(parts, axis=0)

    def placed(first, last):
        rows = arrived(first, last)
        if pieces == near:
            return dot(place_ref[SPAN * tok :, :], rows, ((1,), (0,))).astype(BF16)
        rows = jnp.concatenate([rows, jnp.zeros_like(rows)], axis=0)
        rows = dot(place_ref[SPAN * tok :, :], rows, ((1,), (0,)))
        return (rows + far_ref[:, first:last].astype(F32)).astype(BF16)

    queries = placed(0, width)
    grads = placed(width, base)

    def attend(skipped):
        dead = skipped * tok
        for block in range(skipped, SPAN + 1):
            rows = slice(block * tok, (block + 1) * tok)
            both = dot(place_ref[rows, :], window(block), ((1,), (0,))).astype(BF16)
            key_ref[rows, :] = both[:, :head]
            value_ref[rows, :] = both[:, head:]
        key = key_ref[dead:, :]
        value = value_ref[dead:, :]
        pairs = 4
        mask = jnp.concatenate([mask_ref[dead:, :]] * pairs, axis=1)
        key_grad = jnp.zeros(key.shape, F32)
        value_grad = jnp.zeros(key.shape, F32)
        for first in range(0, heads, pairs):
            spans = [slice(h * head, (h + 1) * head) for h in range(first, first + pairs)]
            q_two = jnp.concatenate([queries[:, s] for s in spans], axis=0)
            g_two = jnp.concatenate([grads[:, s] for s in spans], axis=0)
            scores = dot(key, q_two, ((1,), (1,))) + mask
            top = jnp.max(scores, axis=0, keepdims=True)
            weights = jnp.exp2((scores - top) * factor)
            inverse = 1.0 / jnp.sum(weights, axis=0, keepdims=True)
            prob = weights * inverse
            prob_low = prob.astype(BF16)
            grad_prob = dot(value, g_two, ((1,), (1,)))
            delta = jnp.sum(prob * grad_prob, axis=0, keepdims=True)
            grad_score = (prob * (grad_prob - delta)).astype(BF16)
            value_grad += dot(prob_low, g_two, ((1,), (0,)))
            key_grad += dot(grad_score, q_two, ((1,), (0,)))
            prob_ref[dead:, first * tok : (first + pairs) * tok] = prob_low
            ds_ref[dead:, first * tok : (first + pairs) * tok] = grad_score
        key_grad = key_grad * scale
        for offset, ref in enumerate((own_ref, *part_refs)):
            block = SPAN - offset - skipped
            if block < 0:
                ref[...] = jnp.zeros(ref.shape, ref.dtype)
            else:
                rows = slice(block * tok, (block + 1) * tok)
                ref[:, :head] = key_grad[rows, :].astype(ref.dtype)
                ref[:, head:] = value_grad[rows, :].astype(ref.dtype)

    for_live(live_ref, attend)


def output_kernel(live_ref, key_ref, value_ref, prob_ref, ds_ref, attn_ref, dq_ref):
    tok, width = attn_ref.shape
    head = key_ref.shape[1]
    scale = 1.0 / math.sqrt(head)
    pairs = 4

    def outputs(skipped):
        dead = skipped * tok
        for first in range(0, width // head, pairs):
            cols = slice(first * tok, (first + pairs) * tok)
            out_t = dot(value_ref[dead:, :], prob_ref[dead:, cols], ((0,), (0,)))
            dq_t = dot(key_ref[dead:, :], ds_ref[dead:, cols], ((0,), (0,))) * scale
            for i in range(pairs):
                s = slice((first + i) * head, (first + i + 1) * head)
                attn_ref[:, s] = jnp.transpose(out_t[:, i * tok : (i + 1) * tok]).astype(BF16)
                dq_ref[:, s] = jnp.transpose(dq_t[:, i * tok : (i + 1) * tok]).astype(BF16)

    for_live(live_ref, outputs)


def per_device(query, key, value, grad_out, loader_pos, doc_lengths):
    tok, width = query.shape
    head = key.shape[1]
    devices = lax.axis_size("dcp")
    per_peer = tok // devices
    vmem = pl.BlockSpec(memory_space=pltpu.VMEM)
    params = pltpu.CompilerParams(vmem_limit_bytes=48 << 20)
    hbm = pl.BlockSpec(memory_space=pltpu.HBM)
    base = 2 * width
    paired = devices <= 16 and devices & (devices - 1) == 0
    pieces = devices if paired else 1
    positions = pltpu.with_memory_space_constraint(loader_pos.reshape(devices, tok), pltpu.HBM)
    lengths = pltpu.with_memory_space_constraint(doc_lengths, pltpu.HBM)
    sides = [pltpu.with_memory_space_constraint(x, pltpu.HBM) for x in (query, key, value, grad_out)]
    near = max(1, pieces // 2)
    def swapped(rows, step):
        return lax.ppermute(rows, "dcp", [(d, d ^ step) for d in range(devices)])

    ordered, *packed = pl.pallas_call(
        functools.partial(pack_kernel, per_peer, paired),
        out_shape=[jax.ShapeDtypeStruct((tok, 2 * head), BF16)]
        + [jax.ShapeDtypeStruct((tok // pieces, base), BF16)] * pieces,
        in_specs=[hbm] * 5,
        out_specs=[vmem] * (1 + pieces),
        scratch_shapes=[
            pltpu.VMEM((devices, tok), jnp.int32),
            pltpu.VMEM(key.shape, BF16),
            pltpu.VMEM(value.shape, BF16),
            pltpu.VMEM(query.shape, BF16),
            pltpu.VMEM(grad_out.shape, BF16),
            pltpu.SemaphoreType.DMA((5,)),
        ],
        compiler_params=params,
        name="pack",
    )(positions, sides[1], sides[2], sides[0], sides[3])
    held = [ordered, swapped(ordered, near)] if paired else [ordered]
    for step in range(near, pieces if paired else 0):
        packed[step] = swapped(packed[step], step)
    cols = base + 2 * head * (SPAN + 1) * len(held)
    packed[:near] = pl.pallas_call(
        functools.partial(near_kernel, per_peer, paired, len(held)),
        out_shape=[jax.ShapeDtypeStruct((tok // pieces, cols), BF16)] * near,
        in_specs=[vmem] * (len(held) + near),
        out_specs=[vmem] * near,
        compiler_params=params,
        name="near",
    )(*held, *packed[:near])
    if paired:
        for step in range(1, near):
            packed[step] = swapped(packed[step], step)
    else:
        packed = [lax.all_to_all(packed[0], "dcp", split_axis=0, concat_axis=0, tiled=True)]
    places, mask, live = pl.pallas_call(
        functools.partial(slots_kernel, per_peer, paired),
        out_shape=[
            jax.ShapeDtypeStruct(((SPAN + 1) * tok, tok), BF16),
            jax.ShapeDtypeStruct(((SPAN + 1) * tok, tok), F32),
            jax.ShapeDtypeStruct((8, LANES), F32),
        ],
        in_specs=[hbm, hbm, pl.BlockSpec(memory_space=pl.ANY)],
        out_specs=[vmem] * 3,
        scratch_shapes=[
            pltpu.VMEM((devices, tok), jnp.int32),
            pltpu.SMEM(doc_lengths.shape, jnp.int32),
            pltpu.VMEM((tok, LANES), F32),
            pltpu.SemaphoreType.DMA((2,)),
        ],
        compiler_params=params,
        name="slots",
    )(positions, lengths, packed[0])
    wide = jax.ShapeDtypeStruct((tok, width), BF16)
    if paired:
        far = pl.pallas_call(
            far_kernel,
            out_shape=jax.ShapeDtypeStruct((tok, base), BF16),
            in_specs=[vmem] * (1 + pieces - near),
            out_specs=vmem,
            compiler_params=params,
            cost_estimate=pl.CostEstimate(flops=1 << 33, bytes_accessed=1 << 20, transcendentals=0),
            name="far",
        )(places, *packed[near:])
        packed[near:] = [far]
    rows = (SPAN + 1) * tok
    seen = jax.ShapeDtypeStruct((rows, head), BF16)
    square = jax.ShapeDtypeStruct((rows, tok * width // head), BF16)
    part = jax.ShapeDtypeStruct((tok, 2 * head), BF16)
    keys, values, probs, grad_scores, summed, *parts = pl.pallas_call(
        functools.partial(attend_kernel, width, head, pieces),
        out_shape=[seen, seen, square, square, jax.ShapeDtypeStruct((tok, 2 * head), F32)] + [part] * SPAN,
        in_specs=[vmem] * (3 + len(packed)),
        out_specs=[vmem] * (5 + SPAN),
        compiler_params=params,
        name="attend",
    )(live, mask, places, *packed)
    attn_out, dquery = pl.pallas_call(
        output_kernel,
        out_shape=[wide, wide],
        in_specs=[vmem] * 5,
        out_specs=[vmem] * 2,
        compiler_params=params,
        name="outputs",
    )(live, keys, values, probs, grad_scores)
    for offset in range(SPAN, 0, -1):
        pairs = [(source, source - offset) for source in range(offset, devices)]
        summed = summed + lax.ppermute(parts[offset - 1], "dcp", pairs).astype(F32)
    return attn_out, dquery, summed[:, :head].astype(BF16), summed[:, head:].astype(BF16)


def solution(mesh):
    rows = P(("rep", "dcp"), None)
    return jax.shard_map(
        per_device,
        mesh=mesh,
        in_specs=(rows, rows, rows, rows, P("rep"), P("rep")),
        out_specs=(rows, rows, rows, rows),
        check_vma=False,
    )
```

```python
import functools
import math

import jax
import jax.numpy as jnp
from jax import lax
from jax.experimental import pallas as pl
from jax.experimental.pallas import tpu as pltpu
from jax.sharding import PartitionSpec as P

SPAN = 5
LANES = 128
NEG = -1e30
F32 = jnp.float32
BF16 = jnp.bfloat16


def dot(a, b, dims):
    return lax.dot_general(a, b, (dims, ((), ())), preferred_element_type=F32)


def rank_of(pos_ref, device):
    tok = pos_ref.shape[1]
    pos_row = pos_ref[pl.ds(device, 1), :]
    pos_col = jnp.transpose(jnp.broadcast_to(pos_row, (tok, tok)))
    return pos_row, jnp.sum((pos_col < pos_row).astype(jnp.int32), axis=0, keepdims=True)


def slots_kernel(per_peer, paired, pos_hbm, len_hbm, _, place_ref, mask_ref, live_ref, pos_ref, len_ref, slot_ref, sems):
    copies = [
        pltpu.make_async_copy(pos_hbm, pos_ref, sems.at[0]),
        pltpu.make_async_copy(len_hbm, len_ref, sems.at[1]),
    ]
    for copy in copies:
        copy.start()
    devices, tok = pos_ref.shape
    me = lax.axis_index("dcp")
    rows = (SPAN + 1) * per_peer
    window = (me - SPAN) * per_peer + lax.broadcasted_iota(jnp.int32, (rows, tok), 0)
    lane = lax.broadcasted_iota(jnp.int32, (per_peer, LANES), 1)
    copies[0].wait()

    def slots_from(device):
        pos_row, rank = rank_of(pos_ref, device)
        slot = (pos_row % tok).astype(F32)
        column = jnp.sum(jnp.where(rank == window, slot, 0.0), axis=1, keepdims=True)
        slots = jnp.zeros((per_peer, LANES), F32)
        for block in range(SPAN + 1):
            slots = jnp.where(lane == block, column[block * per_peer : (block + 1) * per_peer], slots)
        return slots

    if devices <= 16:
        for source in range(devices):
            device = source ^ me if paired else source
            slot_ref[source * per_peer : (source + 1) * per_peer, :] = slots_from(device)
    else:

        @pl.loop(0, devices)
        def _(source):
            slot_ref[pl.ds(source * per_peer, per_peer), :] = slots_from(source)

    slot = lax.broadcasted_iota(jnp.int32, (tok, tok), 0).astype(F32)
    arrived = jnp.transpose(slot_ref[...])
    for block in range(SPAN + 1):
        rows = slice(block * tok, (block + 1) * tok)
        place_ref[rows, :] = (arrived[block : block + 1, :] == slot).astype(BF16)

    copies[1].wait()
    q_pos = me * tok + lax.broadcasted_iota(jnp.int32, (1, tok), 1)
    q_start = jnp.zeros((1, tok), jnp.int32)
    end = jnp.int32(0)
    earliest = jnp.int32(0)
    for doc in range(len_ref.shape[0]):
        end = end + len_ref[doc]
        q_start = jnp.where(q_pos >= end, end, q_start)
        earliest = jnp.where(me * tok >= end, end, earliest)
    live_ref[...] = jnp.full(live_ref.shape, me - earliest // tok + 1, jnp.int32).astype(F32)
    k_pos = (me - SPAN) * tok + lax.broadcasted_iota(jnp.int32, mask_ref.shape, 0)
    mask_ref[...] = jnp.where((k_pos >= q_start) & (k_pos <= q_pos), 0.0, NEG)


def group_rows(per_peer, paired, tok):
    want = lax.broadcasted_iota(jnp.int32, (tok, tok), 0)
    if paired:
        want = ((want // per_peer) ^ lax.axis_index("dcp")) * per_peer + want % per_peer
    return want


def pack_kernel(per_peer, paired, pos_hbm, k_hbm, v_hbm, q_hbm, g_hbm, *rest):
    ordered_ref, *out_refs = rest[:-6]
    *targets, sems = rest[-6:]
    copies = [
        pltpu.make_async_copy(source, target, sems.at[i])
        for i, (source, target) in enumerate(zip((pos_hbm, k_hbm, v_hbm, q_hbm, g_hbm), targets))
    ]
    for copy in copies:
        copy.start()
    pos_ref, k_ref, v_ref, q_ref, g_ref = targets
    tok, width = q_ref.shape
    head = k_ref.shape[1]
    step = tok // len(out_refs)
    copies[0].wait()
    rank = rank_of(pos_ref, lax.axis_index("dcp"))[1]
    perm = (rank == lax.broadcasted_iota(jnp.int32, (tok, tok), 0)).astype(BF16)
    for side, ref in enumerate((k_ref, v_ref)):
        copies[1 + side].wait()
        ordered_ref[:, side * head : (side + 1) * head] = dot(perm, ref[...], ((1,), (0,))).astype(BF16)
    perm = (rank == group_rows(per_peer, paired, tok)).astype(BF16)
    for side, ref in enumerate((q_ref, g_ref)):
        copies[3 + side].wait()
        rows = dot(perm, ref[...], ((1,), (0,))).astype(BF16)
        for i, out_ref in enumerate(out_refs):
            out_ref[:, side * width : (side + 1) * width] = rows[i * step : (i + 1) * step]


def near_kernel(per_peer, paired, pairs, *refs):
    pair_refs, refs = refs[:pairs], refs[pairs:]
    near = len(refs) // 2
    step, base = refs[0].shape
    tok, two = pair_refs[0].shape
    want = group_rows(per_peer, paired, tok)[: near * step]
    lane = lax.broadcasted_iota(jnp.int32, want.shape, 1)
    for i in range(near):
        refs[near + i][:, :base] = refs[i][...]
    for block in range(SPAN + 1):
        perm = (lane == want + (block - SPAN) * per_peer).astype(BF16)
        for side, ref in enumerate(pair_refs):
            rows = dot(perm, ref[...], ((1,), (0,))).astype(BF16)
            first = base + two * (side * (SPAN + 1) + block)
            for i in range(near):
                refs[near + i][:, first : first + two] = rows[i * step : (i + 1) * step]


def far_kernel(place_ref, *refs):
    *in_refs, out_ref = refs
    rows = jnp.concatenate([ref[...] for ref in in_refs], axis=0)
    rows = jnp.concatenate([jnp.zeros_like(rows), rows], axis=0)
    out_ref[...] = dot(place_ref[SPAN * out_ref.shape[0] :, :], rows, ((1,), (0,))).astype(BF16)


def for_live(live_ref, body):
    live = jnp.max(live_ref[...])
    pl.when(live > SPAN)(lambda: body(0))
    for skipped in range(1, SPAN + 1):
        pl.when(live == SPAN + 1 - skipped)(functools.partial(body, skipped))


def attend_kernel(width, head, pieces, live_ref, mask_ref, place_ref, *refs):
    near = max(1, pieces // 2)
    in_refs = refs[:near]
    refs = refs[near:]
    if pieces > near:
        far_ref, *refs = refs
    key_ref, value_ref, prob_ref, ds_ref, own_ref, *part_refs = refs
    tok = key_ref.shape[0] // (SPAN + 1)
    heads = width // head
    me = lax.axis_index("dcp")
    scale = 1.0 / math.sqrt(head)
    factor = scale * math.log2(math.e)
    base = 2 * width
    def arrived(first, last):
        return jnp.concatenate([ref[:, first:last] for ref in in_refs], axis=0)

    def window(block):
        parts = []
        for side in range(pieces // near):
            first = base + 2 * head * (side * (SPAN + 1) + block)
            parts += [ref[:, first : first + 2 * head] for ref in in_refs[:near]]
        return jnp.concatenate(parts, axis=0)

    def placed(first, last):
        rows = arrived(first, last)
        if pieces == near:
            return dot(place_ref[SPAN * tok :, :], rows, ((1,), (0,))).astype(BF16)
        rows = jnp.concatenate([rows, jnp.zeros_like(rows)], axis=0)
        rows = dot(place_ref[SPAN * tok :, :], rows, ((1,), (0,)))
        return (rows + far_ref[:, first:last].astype(F32)).astype(BF16)

    queries = placed(0, width)
    grads = placed(width, base)

    def attend(skipped):
        dead = skipped * tok
        for block in range(skipped, SPAN + 1):
            rows = slice(block * tok, (block + 1) * tok)
            both = dot(place_ref[rows, :], window(block), ((1,), (0,))).astype(BF16)
            key_ref[rows, :] = both[:, :head]
            value_ref[rows, :] = both[:, head:]
        key = key_ref[dead:, :]
        value = value_ref[dead:, :]
        pairs = 4
        mask = jnp.concatenate([mask_ref[dead:, :]] * pairs, axis=1)
        key_grad = jnp.zeros(key.shape, F32)
        value_grad = jnp.zeros(key.shape, F32)
        for first in range(0, heads, pairs):
            spans = [slice(h * head, (h + 1) * head) for h in range(first, first + pairs)]
            q_two = jnp.concatenate([queries[:, s] for s in spans], axis=0)
            g_two = jnp.concatenate([grads[:, s] for s in spans], axis=0)
            scores = dot(key, q_two, ((1,), (1,))) + mask
            top = jnp.max(scores, axis=0, keepdims=True)
            weights = jnp.exp2((scores - top) * factor)
            inverse = 1.0 / jnp.sum(weights, axis=0, keepdims=True)
            prob = weights * inverse
            prob_low = prob.astype(BF16)
            grad_prob = dot(value, g_two, ((1,), (1,)))
            delta = jnp.sum(prob * grad_prob, axis=0, keepdims=True)
            grad_score = (prob * (grad_prob - delta)).astype(BF16)
            value_grad += dot(prob_low, g_two, ((1,), (0,)))
            key_grad += dot(grad_score, q_two, ((1,), (0,)))
            prob_ref[dead:, first * tok : (first + pairs) * tok] = prob_low
            ds_ref[dead:, first * tok : (first + pairs) * tok] = grad_score
        key_grad = key_grad * scale
        for offset, ref in enumerate((own_ref, *part_refs)):
            block = SPAN - offset - skipped
            if block < 0:
                ref[...] = jnp.zeros(ref.shape, ref.dtype)
            else:
                rows = slice(block * tok, (block + 1) * tok)
                ref[:, :head] = key_grad[rows, :].astype(ref.dtype)
                ref[:, head:] = value_grad[rows, :].astype(ref.dtype)

    for_live(live_ref, attend)


def output_kernel(live_ref, key_ref, value_ref, prob_ref, ds_ref, attn_ref, dq_ref):
    tok, width = attn_ref.shape
    head = key_ref.shape[1]
    scale = 1.0 / math.sqrt(head)
    pairs = 4

    def outputs(skipped):
        dead = skipped * tok
        for first in range(0, width // head, pairs):
            cols = slice(first * tok, (first + pairs) * tok)
            out_t = dot(value_ref[dead:, :], prob_ref[dead:, cols], ((0,), (0,)))
            dq_t = dot(key_ref[dead:, :], ds_ref[dead:, cols], ((0,), (0,))) * scale
            for i in range(pairs):
                s = slice((first + i) * head, (first + i + 1) * head)
                attn_ref[:, s] = jnp.transpose(out_t[:, i * tok : (i + 1) * tok]).astype(BF16)
                dq_ref[:, s] = jnp.transpose(dq_t[:, i * tok : (i + 1) * tok]).astype(BF16)

    for_live(live_ref, outputs)


def per_device(query, key, value, grad_out, loader_pos, doc_lengths):
    tok, width = query.shape
    head = key.shape[1]
    devices = lax.axis_size("dcp")
    per_peer = tok // devices
    vmem = pl.BlockSpec(memory_space=pltpu.VMEM)
    params = pltpu.CompilerParams(vmem_limit_bytes=48 << 20)
    hbm = pl.BlockSpec(memory_space=pltpu.HBM)
    base = 2 * width
    paired = devices <= 16 and devices & (devices - 1) == 0
    pieces = devices if paired else 1
    positions = pltpu.with_memory_space_constraint(loader_pos.reshape(devices, tok), pltpu.HBM)
    lengths = pltpu.with_memory_space_constraint(doc_lengths, pltpu.HBM)
    sides = [pltpu.with_memory_space_constraint(x, pltpu.HBM) for x in (query, key, value, grad_out)]
    near = max(1, pieces // 2)
    def swapped(rows, step):
        return lax.ppermute(rows, "dcp", [(d, d ^ step) for d in range(devices)])

    ordered, *packed = pl.pallas_call(
        functools.partial(pack_kernel, per_peer, paired),
        out_shape=[jax.ShapeDtypeStruct((tok, 2 * head), BF16)]
        + [jax.ShapeDtypeStruct((tok // pieces, base), BF16)] * pieces,
        in_specs=[hbm] * 5,
        out_specs=[vmem] * (1 + pieces),
        scratch_shapes=[
            pltpu.VMEM((devices, tok), jnp.int32),
            pltpu.VMEM(key.shape, BF16),
            pltpu.VMEM(value.shape, BF16),
            pltpu.VMEM(query.shape, BF16),
            pltpu.VMEM(grad_out.shape, BF16),
            pltpu.SemaphoreType.DMA((5,)),
        ],
        compiler_params=params,
        name="pack",
    )(positions, sides[1], sides[2], sides[0], sides[3])
    held = [ordered, swapped(ordered, near)] if paired else [ordered]
    places, mask, live = pl.pallas_call(
        functools.partial(slots_kernel, per_peer, paired),
        out_shape=[
            jax.ShapeDtypeStruct(((SPAN + 1) * tok, tok), BF16),
            jax.ShapeDtypeStruct(((SPAN + 1) * tok, tok), F32),
            jax.ShapeDtypeStruct((8, LANES), F32),
        ],
        in_specs=[hbm, hbm, pl.BlockSpec(memory_space=pl.ANY)],
        out_specs=[vmem] * 3,
        scratch_shapes=[
            pltpu.VMEM((devices, tok), jnp.int32),
            pltpu.SMEM(doc_lengths.shape, jnp.int32),
            pltpu.VMEM((tok, LANES), F32),
            pltpu.SemaphoreType.DMA((2,)),
        ],
        compiler_params=params,
        name="slots",
    )(positions, lengths, packed[0])
    places, *packed[near + 1 :] = lax.optimization_barrier((places, *packed[near + 1 :]))
    for step in range(near, pieces if paired else 0):
        packed[step] = swapped(packed[step], step)
    cols = base + 2 * head * (SPAN + 1) * len(held)
    packed[:near] = pl.pallas_call(
        functools.partial(near_kernel, per_peer, paired, len(held)),
        out_shape=[jax.ShapeDtypeStruct((tok // pieces, cols), BF16)] * near,
        in_specs=[vmem] * (len(held) + near),
        out_specs=[vmem] * near,
        compiler_params=params,
        name="near",
    )(*held, *packed[:near])
    if paired:
        for step in range(1, near):
            packed[step] = swapped(packed[step], step)
    else:
        packed = [lax.all_to_all(packed[0], "dcp", split_axis=0, concat_axis=0, tiled=True)]
    wide = jax.ShapeDtypeStruct((tok, width), BF16)
    if paired:
        far = pl.pallas_call(
            far_kernel,
            out_shape=jax.ShapeDtypeStruct((tok, base), BF16),
            in_specs=[vmem] * (1 + pieces - near),
            out_specs=vmem,
            compiler_params=params,
            cost_estimate=pl.CostEstimate(flops=1 << 33, bytes_accessed=1 << 20, transcendentals=0),
            name="far",
        )(places, *packed[near:])
        packed[near:] = [far]
    rows = (SPAN + 1) * tok
    seen = jax.ShapeDtypeStruct((rows, head), BF16)
    square = jax.ShapeDtypeStruct((rows, tok * width // head), BF16)
    part = jax.ShapeDtypeStruct((tok, 2 * head), BF16)
    keys, values, probs, grad_scores, summed, *parts = pl.pallas_call(
        functools.partial(attend_kernel, width, head, pieces),
        out_shape=[seen, seen, square, square, jax.ShapeDtypeStruct((tok, 2 * head), F32)] + [part] * SPAN,
        in_specs=[vmem] * (3 + len(packed)),
        out_specs=[vmem] * (5 + SPAN),
        compiler_params=params,
        name="attend",
    )(live, mask, places, *packed)
    attn_out, dquery = pl.pallas_call(
        output_kernel,
        out_shape=[wide, wide],
        in_specs=[vmem] * 5,
        out_specs=[vmem] * 2,
        compiler_params=params,
        name="outputs",
    )(live, keys, values, probs, grad_scores)
    for offset in range(SPAN, 0, -1):
        pairs = [(source, source - offset) for source in range(offset, devices)]
        summed = summed + lax.ppermute(parts[offset - 1], "dcp", pairs).astype(F32)
    return attn_out, dquery, summed[:, :head].astype(BF16), summed[:, head:].astype(BF16)


def solution(mesh):
    rows = P(("rep", "dcp"), None)
    return jax.shard_map(
        per_device,
        mesh=mesh,
        in_specs=(rows, rows, rows, rows, P("rep"), P("rep")),
        out_specs=(rows, rows, rows, rows),
        check_vma=False,
    )
```

```python
import functools
import math

import jax
import jax.numpy as jnp
from jax import lax
from jax.experimental import pallas as pl
from jax.experimental.pallas import tpu as pltpu
from jax.sharding import PartitionSpec as P

SPAN = 5
LANES = 128
NEG = -1e30
F32 = jnp.float32
BF16 = jnp.bfloat16


def dot(a, b, dims):
    return lax.dot_general(a, b, (dims, ((), ())), preferred_element_type=F32)


def rank_of(pos_ref, device):
    tok = pos_ref.shape[1]
    pos_row = pos_ref[pl.ds(device, 1), :]
    pos_col = jnp.transpose(jnp.broadcast_to(pos_row, (tok, tok)))
    return pos_row, jnp.sum((pos_col < pos_row).astype(jnp.int32), axis=0, keepdims=True)


def slots_kernel(per_peer, paired, pos_hbm, len_hbm, _, place_ref, mask_ref, live_ref, pos_ref, len_ref, slot_ref, sems):
    copies = [
        pltpu.make_async_copy(pos_hbm, pos_ref, sems.at[0]),
        pltpu.make_async_copy(len_hbm, len_ref, sems.at[1]),
    ]
    for copy in copies:
        copy.start()
    devices, tok = pos_ref.shape
    me = lax.axis_index("dcp")
    rows = (SPAN + 1) * per_peer
    window = (me - SPAN) * per_peer + lax.broadcasted_iota(jnp.int32, (rows, tok), 0)
    lane = lax.broadcasted_iota(jnp.int32, (per_peer, LANES), 1)
    copies[0].wait()

    def slots_from(device):
        pos_row, rank = rank_of(pos_ref, device)
        slot = (pos_row % tok).astype(F32)
        column = jnp.sum(jnp.where(rank == window, slot, 0.0), axis=1, keepdims=True)
        slots = jnp.zeros((per_peer, LANES), F32)
        for block in range(SPAN + 1):
            slots = jnp.where(lane == block, column[block * per_peer : (block + 1) * per_peer], slots)
        return slots

    if devices <= 16:
        for source in range(devices):
            device = source ^ me if paired else source
            slot_ref[source * per_peer : (source + 1) * per_peer, :] = slots_from(device)
    else:

        @pl.loop(0, devices)
        def _(source):
            slot_ref[pl.ds(source * per_peer, per_peer), :] = slots_from(source)

    slot = lax.broadcasted_iota(jnp.int32, (tok, tok), 0).astype(F32)
    arrived = jnp.transpose(slot_ref[...])
    for block in range(SPAN + 1):
        rows = slice(block * tok, (block + 1) * tok)
        place_ref[rows, :] = (arrived[block : block + 1, :] == slot).astype(BF16)

    copies[1].wait()
    q_pos = me * tok + lax.broadcasted_iota(jnp.int32, (1, tok), 1)
    q_start = jnp.zeros((1, tok), jnp.int32)
    end = jnp.int32(0)
    earliest = jnp.int32(0)
    for doc in range(len_ref.shape[0]):
        end = end + len_ref[doc]
        q_start = jnp.where(q_pos >= end, end, q_start)
        earliest = jnp.where(me * tok >= end, end, earliest)
    live_ref[...] = jnp.full(live_ref.shape, me - earliest // tok + 1, jnp.int32).astype(F32)
    k_pos = (me - SPAN) * tok + lax.broadcasted_iota(jnp.int32, mask_ref.shape, 0)
    mask_ref[...] = jnp.where((k_pos >= q_start) & (k_pos <= q_pos), 0.0, NEG)


def group_rows(per_peer, paired, tok):
    want = lax.broadcasted_iota(jnp.int32, (tok, tok), 0)
    if paired:
        want = ((want // per_peer) ^ lax.axis_index("dcp")) * per_peer + want % per_peer
    return want


def pack_kernel(per_peer, paired, pos_hbm, k_hbm, v_hbm, q_hbm, g_hbm, *rest):
    ordered_ref, *out_refs = rest[:-6]
    *targets, sems = rest[-6:]
    copies = [
        pltpu.make_async_copy(source, target, sems.at[i])
        for i, (source, target) in enumerate(zip((pos_hbm, k_hbm, v_hbm, q_hbm, g_hbm), targets))
    ]
    for copy in copies:
        copy.start()
    pos_ref, k_ref, v_ref, q_ref, g_ref = targets
    tok, width = q_ref.shape
    head = k_ref.shape[1]
    step = tok // len(out_refs)
    copies[0].wait()
    rank = rank_of(pos_ref, lax.axis_index("dcp"))[1]
    perm = (rank == lax.broadcasted_iota(jnp.int32, (tok, tok), 0)).astype(BF16)
    for side, ref in enumerate((k_ref, v_ref)):
        copies[1 + side].wait()
        ordered_ref[:, side * head : (side + 1) * head] = dot(perm, ref[...], ((1,), (0,))).astype(BF16)
    perm = (rank == group_rows(per_peer, paired, tok)).astype(BF16)
    for side, ref in enumerate((q_ref, g_ref)):
        copies[3 + side].wait()
        rows = dot(perm, ref[...], ((1,), (0,))).astype(BF16)
        for i, out_ref in enumerate(out_refs):
            out_ref[:, side * width : (side + 1) * width] = rows[i * step : (i + 1) * step]


def near_kernel(per_peer, paired, pairs, *refs):
    pair_refs, refs = refs[:pairs], refs[pairs:]
    near = len(refs) // 2
    step, base = refs[0].shape
    tok, two = pair_refs[0].shape
    want = group_rows(per_peer, paired, tok)[: near * step]
    lane = lax.broadcasted_iota(jnp.int32, want.shape, 1)
    for i in range(near):
        refs[near + i][:, :base] = refs[i][...]
    for block in range(SPAN + 1):
        perm = (lane == want + (block - SPAN) * per_peer).astype(BF16)
        for side, ref in enumerate(pair_refs):
            rows = dot(perm, ref[...], ((1,), (0,))).astype(BF16)
            first = base + two * (side * (SPAN + 1) + block)
            for i in range(near):
                refs[near + i][:, first : first + two] = rows[i * step : (i + 1) * step]


def far_kernel(place_ref, *refs):
    *in_refs, out_ref = refs
    rows = jnp.concatenate([ref[...] for ref in in_refs], axis=0)
    rows = jnp.concatenate([jnp.zeros_like(rows), rows], axis=0)
    out_ref[...] = dot(place_ref[SPAN * out_ref.shape[0] :, :], rows, ((1,), (0,))).astype(BF16)


def for_live(live_ref, body):
    live = jnp.max(live_ref[...])
    pl.when(live > SPAN)(lambda: body(0))
    for skipped in range(1, SPAN + 1):
        pl.when(live == SPAN + 1 - skipped)(functools.partial(body, skipped))


def attend_kernel(width, head, pieces, live_ref, mask_ref, place_ref, *refs):
    near = max(1, pieces // 2)
    in_refs = refs[:near]
    refs = refs[near:]
    if pieces > near:
        far_ref, *refs = refs
    key_ref, value_ref, prob_ref, ds_ref, own_ref, *part_refs = refs
    tok = key_ref.shape[0] // (SPAN + 1)
    heads = width // head
    me = lax.axis_index("dcp")
    scale = 1.0 / math.sqrt(head)
    factor = scale * math.log2(math.e)
    base = 2 * width
    def arrived(first, last):
        return jnp.concatenate([ref[:, first:last] for ref in in_refs], axis=0)

    def window(block):
        parts = []
        for side in range(pieces // near):
            first = base + 2 * head * (side * (SPAN + 1) + block)
            parts += [ref[:, first : first + 2 * head] for ref in in_refs[:near]]
        return jnp.concatenate(parts, axis=0)

    def placed(first, last):
        rows = arrived(first, last)
        if pieces == near:
            return dot(place_ref[SPAN * tok :, :], rows, ((1,), (0,))).astype(BF16)
        rows = jnp.concatenate([rows, jnp.zeros_like(rows)], axis=0)
        rows = dot(place_ref[SPAN * tok :, :], rows, ((1,), (0,)))
        return (rows + far_ref[:, first:last].astype(F32)).astype(BF16)

    queries = placed(0, width)
    grads = placed(width, base)

    def attend(skipped):
        dead = skipped * tok
        for block in range(skipped, SPAN + 1):
            rows = slice(block * tok, (block + 1) * tok)
            both = dot(place_ref[rows, :], window(block), ((1,), (0,))).astype(BF16)
            key_ref[rows, :] = both[:, :head]
            value_ref[rows, :] = both[:, head:]
        key = key_ref[dead:, :]
        value = value_ref[dead:, :]
        pairs = 4
        mask = jnp.concatenate([mask_ref[dead:, :]] * pairs, axis=1)
        key_grad = jnp.zeros(key.shape, F32)
        value_grad = jnp.zeros(key.shape, F32)
        for first in range(0, heads, pairs):
            spans = [slice(h * head, (h + 1) * head) for h in range(first, first + pairs)]
            q_two = jnp.concatenate([queries[:, s] for s in spans], axis=0)
            g_two = jnp.concatenate([grads[:, s] for s in spans], axis=0)
            scores = dot(key, q_two, ((1,), (1,))) + mask
            top = jnp.max(scores, axis=0, keepdims=True)
            weights = jnp.exp2((scores - top) * factor)
            inverse = 1.0 / jnp.sum(weights, axis=0, keepdims=True)
            prob = weights * inverse
            prob_low = prob.astype(BF16)
            grad_prob = dot(value, g_two, ((1,), (1,)))
            delta = jnp.sum(prob * grad_prob, axis=0, keepdims=True)
            grad_score = (prob * (grad_prob - delta)).astype(BF16)
            value_grad += dot(prob_low, g_two, ((1,), (0,)))
            key_grad += dot(grad_score, q_two, ((1,), (0,)))
            prob_ref[dead:, first * tok : (first + pairs) * tok] = prob_low
            ds_ref[dead:, first * tok : (first + pairs) * tok] = grad_score
        key_grad = key_grad * scale
        for offset, ref in enumerate((own_ref, *part_refs)):
            block = SPAN - offset - skipped
            if block < 0:
                ref[...] = jnp.zeros(ref.shape, ref.dtype)
            else:
                rows = slice(block * tok, (block + 1) * tok)
                ref[:, :head] = key_grad[rows, :].astype(ref.dtype)
                ref[:, head:] = value_grad[rows, :].astype(ref.dtype)

    for_live(live_ref, attend)


def output_kernel(live_ref, key_ref, value_ref, prob_ref, ds_ref, attn_ref, dq_ref):
    tok, width = attn_ref.shape
    head = key_ref.shape[1]
    scale = 1.0 / math.sqrt(head)
    pairs = 4

    def outputs(skipped):
        dead = skipped * tok
        for first in range(0, width // head, pairs):
            cols = slice(first * tok, (first + pairs) * tok)
            out_t = dot(value_ref[dead:, :], prob_ref[dead:, cols], ((0,), (0,)))
            dq_t = dot(key_ref[dead:, :], ds_ref[dead:, cols], ((0,), (0,))) * scale
            for i in range(pairs):
                s = slice((first + i) * head, (first + i + 1) * head)
                attn_ref[:, s] = jnp.transpose(out_t[:, i * tok : (i + 1) * tok]).astype(BF16)
                dq_ref[:, s] = jnp.transpose(dq_t[:, i * tok : (i + 1) * tok]).astype(BF16)

    for_live(live_ref, outputs)


def per_device(query, key, value, grad_out, loader_pos, doc_lengths):
    tok, width = query.shape
    head = key.shape[1]
    devices = lax.axis_size("dcp")
    per_peer = tok // devices
    vmem = pl.BlockSpec(memory_space=pltpu.VMEM)
    params = pltpu.CompilerParams(vmem_limit_bytes=48 << 20)
    hbm = pl.BlockSpec(memory_space=pltpu.HBM)
    base = 2 * width
    paired = devices <= 16 and devices & (devices - 1) == 0
    pieces = devices if paired else 1
    positions = pltpu.with_memory_space_constraint(loader_pos.reshape(devices, tok), pltpu.HBM)
    lengths = pltpu.with_memory_space_constraint(doc_lengths, pltpu.HBM)
    sides = [pltpu.with_memory_space_constraint(x, pltpu.HBM) for x in (query, key, value, grad_out)]
    near = max(1, pieces // 2)
    def swapped(rows, step):
        return lax.ppermute(rows, "dcp", [(d, d ^ step) for d in range(devices)])

    ordered, *packed = pl.pallas_call(
        functools.partial(pack_kernel, per_peer, paired),
        out_shape=[jax.ShapeDtypeStruct((tok, 2 * head), BF16)]
        + [jax.ShapeDtypeStruct((tok // pieces, base), BF16)] * pieces,
        in_specs=[hbm] * 5,
        out_specs=[vmem] * (1 + pieces),
        scratch_shapes=[
            pltpu.VMEM((devices, tok), jnp.int32),
            pltpu.VMEM(key.shape, BF16),
            pltpu.VMEM(value.shape, BF16),
            pltpu.VMEM(query.shape, BF16),
            pltpu.VMEM(grad_out.shape, BF16),
            pltpu.SemaphoreType.DMA((5,)),
        ],
        compiler_params=params,
        name="pack",
    )(positions, sides[1], sides[2], sides[0], sides[3])
    held = [ordered, swapped(ordered, near)] if paired else [ordered]
    for step in range(near, pieces if paired else 0):
        packed[step] = swapped(packed[step], step)
    cols = base + 2 * head * (SPAN + 1) * len(held)
    packed[:near] = pl.pallas_call(
        functools.partial(near_kernel, per_peer, paired, len(held)),
        out_shape=[jax.ShapeDtypeStruct((tok // pieces, cols), BF16)] * near,
        in_specs=[vmem] * (len(held) + near),
        out_specs=[vmem] * near,
        compiler_params=params,
        name="near",
    )(*held, *packed[:near])
    if paired:
        for step in range(1, near):
            packed[step] = swapped(packed[step], step)
    else:
        packed = [lax.all_to_all(packed[0], "dcp", split_axis=0, concat_axis=0, tiled=True)]
    places, mask, live = pl.pallas_call(
        functools.partial(slots_kernel, per_peer, paired),
        out_shape=[
            jax.ShapeDtypeStruct(((SPAN + 1) * tok, tok), BF16),
            jax.ShapeDtypeStruct(((SPAN + 1) * tok, tok), F32),
            jax.ShapeDtypeStruct((8, LANES), F32),
        ],
        in_specs=[hbm, hbm, pl.BlockSpec(memory_space=pl.ANY)],
        out_specs=[vmem] * 3,
        scratch_shapes=[
            pltpu.VMEM((devices, tok), jnp.int32),
            pltpu.SMEM(doc_lengths.shape, jnp.int32),
            pltpu.VMEM((tok, LANES), F32),
            pltpu.SemaphoreType.DMA((2,)),
        ],
        compiler_params=params,
        name="slots",
    )(positions, lengths, packed[0])
    wide = jax.ShapeDtypeStruct((tok, width), BF16)
    if paired:
        far = pl.pallas_call(
            far_kernel,
            out_shape=jax.ShapeDtypeStruct((tok, base), BF16),
            in_specs=[vmem] * (1 + pieces - near),
            out_specs=vmem,
            compiler_params=params,
            cost_estimate=pl.CostEstimate(flops=1 << 33, bytes_accessed=1 << 20, transcendentals=0),
            name="far",
        )(places, *packed[near:])
        packed[near:] = [far]
    rows = (SPAN + 1) * tok
    seen = jax.ShapeDtypeStruct((rows, head), BF16)
    square = jax.ShapeDtypeStruct((rows, tok * width // head), BF16)
    part = jax.ShapeDtypeStruct((tok, 2 * head), BF16)
    keys, values, probs, grad_scores, summed, *parts = pl.pallas_call(
        functools.partial(attend_kernel, width, head, pieces),
        out_shape=[seen, seen, square, square, jax.ShapeDtypeStruct((tok, 2 * head), F32)] + [part] * SPAN,
        in_specs=[vmem] * (3 + len(packed)),
        out_specs=[vmem] * (5 + SPAN),
        compiler_params=params,
        name="attend",
    )(live, mask, places, *packed)
    attn_out, dquery = pl.pallas_call(
        output_kernel,
        out_shape=[wide, wide],
        in_specs=[vmem] * 5,
        out_specs=[vmem] * 2,
        compiler_params=params,
        name="outputs",
    )(live, keys, values, probs, grad_scores)
    for offset in (4, 5, 3, 2, 1):
        pairs = [(source, source - offset) for source in range(offset, devices)]
        summed = summed + lax.ppermute(parts[offset - 1], "dcp", pairs).astype(F32)
    return attn_out, dquery, summed[:, :head].astype(BF16), summed[:, head:].astype(BF16)


def solution(mesh):
    rows = P(("rep", "dcp"), None)
    return jax.shard_map(
        per_device,
        mesh=mesh,
        in_specs=(rows, rows, rows, rows, P("rep"), P("rep")),
        out_specs=(rows, rows, rows, rows),
        check_vma=False,
    )
```
